512 devices in a mesh: rows: 128 (over z, y_hi, x, core), heads: 4 (over y_lo).
Axes of the slice: x: 4, y: 8 (y_hi: 2, y_lo: 4; y = y_hi * 4 + y_lo), z: 8, core: 2. Of those that a mesh axis runs over, the one named last changes fastest.
Arguments:
- features: bfloat16 [1024, 128, 384], P('heads', 'rows'), may hold values from -6 to 6
- cotangent: bfloat16 [1024, 128, 384], P('heads', 'rows'), may hold values from -0.59765625 to 0.59765625
- inject_row: bfloat16 [64, 128, 384], P(None, 'rows'), may hold values from -0.75 to 0.75
- readout_row: bfloat16 [64, 128, 384], P(None, 'rows'), may hold values from -3 to 3
- inject_col: bfloat16 [64, 128, 384], P(None, 'rows'), may hold values from -0.75 to 0.75
- readout_col: bfloat16 [64, 128, 384], P(None, 'rows'), may hold values from -3 to 3
- decay_row: bfloat16 [16, 128, 384], P('heads', 'rows'), may hold values from -0.8 to 0
- decay_col: bfloat16 [16, 128, 384], P('heads', 'rows'), may hold values from -0.8 to 0
- tissue: int32 [128, 24], P('rows'), may hold values 0 or 1
Outputs:
- grad_features: bfloat16 [1024, 128, 384], P('heads', 'rows')
- grad_inject_row: bfloat16 [64, 128, 384], P('heads', 'rows')
- grad_readout_row: bfloat16 [64, 128, 384], P('heads', 'rows')
- grad_inject_col: bfloat16 [64, 128, 384], P('heads', 'rows')
- grad_readout_col: bfloat16 [64, 128, 384], P('heads', 'rows')
- grad_decay_row: bfloat16 [16, 128, 384], P('heads', 'rows')
- grad_decay_col: bfloat16 [16, 128, 384], P('heads', 'rows')
The draws below stay inside these ranges and needn't reach their ends.
All inputs are finite; a program needn't handle non-finite values. No bound on the sum of `tissue` on one device may be relied on, other than what follows from the above.
Results may differ from the reference program's by a relative error of at most 0.005.
Values may be sent and summed in bfloat16 or wider, within the bound.
No kernel may reach another device: no remote copies, remote signals or barrier semaphores. Data moves between devices by JAX's collectives and lax.ppermute only.
A program may use at most 64 MiB of HBM per device.

```python
import math
from functools import partial
import jax
import jax.numpy as jnp
from jax import lax

HEADS = 16
HEAD_DIM = 64
STATE = 64
SPAN = 128
TILE = 16
R_DEV = 1
COLS = 384
CHAN = 1024
ROWS = 128
N_ROWS = 128


def decay_draw(key, chained_order):
    noise_seeds = jax.random.split(key, 4)
    lowest = math.log(1.0 / (8.0 * chained_order))
    highest = math.log(1.0 / 30.0)
    tensor_extent = (HEADS, ROWS, COLS)
    update_factor = jnp.exp(jax.random.uniform(noise_seeds[0], (HEADS, 1, 1), jnp.float32, lowest, highest))
    advance_spacing = jnp.exp(jax.random.uniform(noise_seeds[1], tensor_extent, jnp.float32, math.log(0.5), math.log(2.0)))
    transfer_bundles = jax.random.uniform(noise_seeds[2], tensor_extent, jnp.float32) < 2.0 / chained_order
    objective_trace = jax.random.uniform(noise_seeds[3], tensor_extent, jnp.float32, 0.22, 0.6)
    return -(update_factor * advance_spacing) - jnp.where(transfer_bundles, objective_trace, 0.0)


def draw_decay_row(key, part):
    return decay_draw(jax.random.fold_in(key, 11), COLS).astype(jnp.bfloat16)


def draw_decay_col(key, part):
    return decay_draw(jax.random.fold_in(key, 23), ROWS).astype(jnp.bfloat16)


def plant(values, key, low, largest):
    extent = values.shape
    place = [jax.random.randint(jax.random.fold_in(key, axis), (), 0, extent[axis]) for axis in range(len(extent))]
    values = values.at[tuple(place)].set(low)
    longest = extent.index(max(extent))
    place[longest] = (place[longest] + 1) % extent[longest]
    return values.at[tuple(place)].set(largest)


def steps_of(own_key, dims, cuts, smallest, top_value):
    gain, own = 1.0, jax.random.fold_in(own_key, 6)
    for dim, blocks in cuts:
        heights = jnp.exp(jax.random.uniform(jax.random.fold_in(own, dim), (blocks,), jnp.float32, smallest / len(cuts), top_value / len(cuts)))
        gain = gain * jnp.repeat(heights, dims[dim] // blocks).reshape([-1 if axis == dim else 1 for axis in range(len(dims))])
    return gain


def gaussian(own_key, extent, scale, reach, cuts=(), kind=jnp.bfloat16):
    values = scale * jax.random.normal(own_key, extent, jnp.float32)
    if cuts:
        values = values * steps_of(own_key, extent, cuts, -0.22, 0.18)
    return jnp.clip(values, -reach, reach).astype(kind)


def setup_inputs(seed: int = 0) -> dict:
    key_list = jax.random.split(jax.random.key(seed), 10)
    return {
        "features": gaussian(key_list[0], (CHAN, ROWS, COLS), 1.0, 6.0, ((0, 4), (1, 128))),
        "cotangent": gaussian(key_list[1], (CHAN, ROWS, COLS), 0.1, 0.59765625, ((0, 4), (1, 128))),
        "inject_row": gaussian(key_list[2], (STATE, ROWS, COLS), 0.125, 0.75, ((1, 128),)),
        "readout_row": gaussian(key_list[3], (STATE, ROWS, COLS), 0.5, 3.0, ((1, 128),)),
        "inject_col": gaussian(key_list[4], (STATE, ROWS, COLS), 0.125, 0.75, ((1, 128),)),
        "readout_col": gaussian(key_list[5], (STATE, ROWS, COLS), 0.5, 3.0, ((1, 128),)),
        "decay_row": draw_decay_row(jax.random.fold_in(key_list[9], 71), 0),
        "decay_col": draw_decay_col(jax.random.fold_in(key_list[9], 71), 0),
        "tissue": plant((jax.random.randint(key_list[8], (ROWS, COLS // TILE), 0, 4) < 3).astype(jnp.int32), jax.random.fold_in(key_list[8], 1), 0, 1),
    }


HIGHEST = lax.Precision.HIGHEST

def objective(values, weights, inject, readout, log_decay, block_len):
    heads_here, head_size, seq_count, length = values.shape
    nstate = inject.shape[0]
    blocks = length // block_len
    values_b = values.reshape(heads_here, head_size, seq_count, blocks, block_len)
    weights_b = weights.reshape(heads_here, head_size, seq_count, blocks, block_len)
    inject_b = inject.reshape(nstate, seq_count, blocks, block_len)
    readout_b = readout.reshape(nstate, seq_count, blocks, block_len)
    decay_b = log_decay.reshape(heads_here, seq_count, blocks, block_len)
    running = jnp.cumsum(decay_b, axis=-1)
    lower_mask = jnp.tril(jnp.ones((block_len, block_len), dtype=bool))
    spread = running[..., :, None] - running[..., None, :]
    within = jnp.where(lower_mask, jnp.exp(jnp.where(lower_mask, spread, 0.0)), 0.0)
    intersection = jnp.einsum('nskt,nsku->sktu', readout_b, inject_b, precision=HIGHEST)
    pairing = jnp.einsum('hpskt,hpsku->hsktu', weights_b, values_b, precision=HIGHEST)
    inner = jnp.sum(within * intersection[None] * pairing)
    to_end = jnp.exp(running[..., -1:] - running)
    local_state = jnp.einsum('nsku,hsku,hpsku->hsknp', inject_b, to_end, values_b, precision=HIGHEST)
    block_sum = running[..., -1]
    through = jnp.cumsum(block_sum, axis=-1)
    before_block = through - block_sum
    earlier_mask = jnp.tril(jnp.ones((blocks, blocks), dtype=bool), -1)
    between = before_block[..., :, None] - through[..., None, :]
    carry_weight = jnp.where(earlier_mask, jnp.exp(jnp.where(earlier_mask, between, 0.0)), 0.0)
    carried = jnp.einsum('hskj,hsjnp->hsknp', carry_weight, local_state, precision=HIGHEST)
    emitted = jnp.einsum('nskt,hsknp->hpskt', readout_b, carried, precision=HIGHEST)
    outer = jnp.sum(weights_b * jnp.exp(running)[:, None] * emitted)
    return inner + outer

def grads_of(values, weights, inject, readout, log_decay):
    block_len = min(SPAN, values.shape[-1])
    return jax.grad(partial(objective, block_len=block_len), argnums=(0, 2, 3, 4))(values, weights, inject, readout, log_decay)

def cut_groups(array, group):
    tensor_extent = array.shape
    return jnp.moveaxis(array.reshape(tensor_extent[:-2] + (tensor_extent[-2] // group, group, tensor_extent[-1])), -3, 0)

def join_groups(array):
    moved = jnp.moveaxis(array, 0, -3)
    tensor_extent = moved.shape
    return moved.reshape(tensor_extent[:-3] + (tensor_extent[-3] * tensor_extent[-2], tensor_extent[-1]))

def blockwise(values, weights, inject, readout, log_decay, group):
    pieces = (cut_groups(values, group), cut_groups(weights, group), cut_groups(inject, group), cut_groups(readout, group), cut_groups(log_decay, group))
    result = lax.map(lambda parts: grads_of(parts[0], parts[1], parts[2], parts[3], parts[4]), pieces)
    return tuple((join_groups(item) for item in result))

def reference(features, cotangent, inject_row, readout_row, inject_col, readout_col, decay_row, decay_col, tissue):
    tissue_keep = jnp.repeat(tissue, TILE, axis=1).astype(jnp.bfloat16)
    kept_features = (features * tissue_keep[None]).astype(jnp.float32).reshape(HEADS, HEAD_DIM, ROWS, COLS)
    kept_cotangent = (cotangent * tissue_keep[None]).astype(jnp.float32).reshape(HEADS, HEAD_DIM, ROWS, COLS)
    row_grads = blockwise(kept_features, kept_cotangent, inject_row.astype(jnp.float32), readout_row.astype(jnp.float32), decay_row.astype(jnp.float32), R_DEV)
    col_grads = blockwise(kept_features.transpose(0, 1, 3, 2), kept_cotangent.transpose(0, 1, 3, 2), inject_col.astype(jnp.float32).transpose(0, 2, 1), readout_col.astype(jnp.float32).transpose(0, 2, 1), decay_col.astype(jnp.float32).transpose(0, 2, 1), COLS // N_ROWS)
    col_values = lax.optimization_barrier(col_grads[0].transpose(0, 1, 3, 2).astype(jnp.bfloat16)).astype(jnp.float32)
    grad_features = ((row_grads[0] + col_values).reshape(CHAN, ROWS, COLS) * tissue_keep[None]).astype(jnp.bfloat16)
    grad_inject_row = row_grads[1].astype(jnp.bfloat16)
    grad_readout_row = row_grads[2].astype(jnp.bfloat16)
    grad_inject_col = col_grads[1].transpose(0, 2, 1).astype(jnp.bfloat16)
    grad_readout_col = col_grads[2].transpose(0, 2, 1).astype(jnp.bfloat16)
    grad_decay_row = row_grads[3].astype(jnp.bfloat16)
    grad_decay_col = col_grads[3].transpose(0, 2, 1).astype(jnp.bfloat16)
    return (grad_features, grad_inject_row, grad_readout_row, grad_inject_col, grad_readout_col, grad_decay_row, grad_decay_col)
```

```python
from functools import partial

import jax
import jax.numpy as jnp
from jax import lax
from jax.experimental import pallas as pl
from jax.experimental.pallas import tpu as pltpu
from jax.sharding import PartitionSpec as P

TILE = 16
L = 128
HD = 64
F32, BF16 = jnp.float32, jnp.bfloat16


def nn(a, b):
    return lax.dot_general(a, b, (((1,), (0,)), ((), ())), preferred_element_type=F32)


def nt(a, b):
    return lax.dot_general(a, b, (((1,), (1,)), ((), ())), preferred_element_type=F32)


def tn(a, b):
    return lax.dot_general(a, b, (((0,), (0,)), ((), ())), preferred_element_type=F32)


def upper(dtype):
    i = lax.broadcasted_iota(jnp.int32, (L, L), 0)
    j = lax.broadcasted_iota(jnp.int32, (L, L), 1)
    return (i <= j).astype(dtype)


def split3(x):
    hi = x.astype(BF16)
    r = x - hi.astype(F32)
    mid = r.astype(BF16)
    return hi, mid, (r - mid.astype(F32)).astype(BF16)


def keep_of(tissue, n):
    tiles = tissue.shape[1]
    t = lax.broadcasted_iota(jnp.int32, (tiles, n), 0) * TILE
    j = lax.broadcasted_iota(jnp.int32, (tiles, n), 1)
    spread = ((j >= t) & (j < t + TILE)).astype(F32)
    rows = jnp.broadcast_to(tissue.astype(F32), (8, tiles))
    return nn(rows, spread)[0:1]


def prep_kernel(x_ref, w_ref, u_ref, v_ref, a_ref, tis_ref, send_ref, xm_ref, wm_ref, wt_ref, scr):
    n = x_ref.shape[1]
    blocks = n // L
    keep = keep_of(tis_ref[...], n).astype(BF16)
    xm_ref[...] = x_ref[...] * keep
    wm_ref[...] = w_ref[...] * keep
    halves = x_ref.shape[0] // L
    per = 2 * halves + 1
    for k in range(blocks):
        at = pl.ds(k * L, L)
        for r in range(halves):
            ch = pl.ds(r * L, L)
            scr[:, per * k + r, :] = xm_ref[ch, at].astype(F32).T
            wt = wm_ref[ch, at].astype(F32).T
            scr[:, per * k + halves + r, :] = wt
            wt_ref[at, ch] = wt.astype(BF16)
        uv = jnp.concatenate([u_ref[:, at].astype(F32), v_ref[:, at].astype(F32)], axis=0)
        scr[:, per * k + 2 * halves, :] = uv.T
    heads = a_ref.shape[0]
    a = [a_ref[:, pl.ds(k * L, L)].astype(F32) for k in range(blocks)]
    a.append(jnp.zeros((L - heads * blocks, L), F32))
    scr[:, per * blocks, :] = jnp.concatenate(a, axis=0).T
    send_ref[...] = scr[...].astype(BF16)


def row_kernel(xm_ref, wm_ref, wt_ref, u_ref, v_ref, a_ref, dx_ref, d0_ref, d1_ref, d2_ref, d3_ref, da_ref, y_ref, duv_ref):
    n = xm_ref.shape[1]
    blocks = n // L
    heads = a_ref.shape[0]
    nstate = u_ref.shape[0]
    tri = upper(BF16)
    le = upper(F32)
    carry = jnp.zeros((heads, 1), F32)
    grow, gcol = [], []
    for b in range(blocks):
        g = nn(a_ref[:, pl.ds(b * L, L)], tri) + carry
        carry = g[:, L - 1 : L]
        grow.append(g)
        gcol.append(jnp.concatenate([g, jnp.zeros((8 - heads, L), F32)], axis=0).T)
    vt = [v_ref[:, pl.ds(b * L, L)].astype(F32).T.astype(BF16) for b in range(blocks)]
    i0 = lax.broadcasted_iota(jnp.int32, (L, L), 0)
    i1 = lax.broadcasted_iota(jnp.int32, (L, L), 1)
    lower = i1 <= i0
    dv = [None] * blocks
    du = [None] * blocks
    for j in range(blocks):
        sj = pl.ds(j * L, L)
        dxs = [None] * heads
        for i in range(j, blocks):
            ti = pl.ds(i * L, L)
            s = nn(vt[i], u_ref[:, sj])
            q = None
            for h in range(heads):
                ch = pl.ds(h * HD, HD)
                d = jnp.exp(jnp.minimum(gcol[i][:, h : h + 1] - grow[j][h : h + 1, :], 0.0))
                if i == j:
                    d = jnp.where(lower, d, 0.0)
                m = nn(wt_ref[ti, ch], xm_ref[ch, sj])
                dm = d * m
                q = dm if q is None else q + dm
                a = (d * s).astype(BF16)
                part = nn(wm_ref[ch, ti], a)
                dxs[h] = part if dxs[h] is None else dxs[h] + part
                y = nt(xm_ref[ch, sj], a)
                if j == 0:
                    y_ref[ch, ti] = y
                else:
                    y_ref[ch, ti] += y
            qb = q.astype(BF16)
            pu = nn(v_ref[:, ti], qb)
            pv = nt(u_ref[:, sj], qb)
            du[j] = pu if du[j] is None else du[j] + pu
            dv[i] = pv if dv[i] is None else dv[i] + pv
        for h in range(heads):
            dx_ref[pl.ds(h * HD, HD), sj] = dxs[h]
    quarter = nstate // 4
    for b in range(blocks):
        at = pl.ds(b * L, L)
        for k in range(4):
            duv_ref[pl.ds(2 * quarter * k, quarter), at] = du[b][quarter * k : quarter * (k + 1)]
            duv_ref[pl.ds(2 * quarter * k + quarter, quarter), at] = dv[b][quarter * k : quarter * (k + 1)]
    me = lax.axis_index("heads")
    for shift, ref in enumerate((d0_ref, d1_ref, d2_ref, d3_ref)):
        part = lax.rem(me + shift, 4) * (2 * quarter)
        ref[...] = duv_ref[pl.ds(pl.multiple_of(part, 2 * quarter), 2 * quarter), :].astype(ref.dtype)
    suffix = (i0 >= i1).astype(BF16)
    later = jnp.zeros((heads, 1), F32)
    for b in reversed(range(blocks)):
        at = pl.ds(b * L, L)
        e = wm_ref[:, at].astype(F32) * y_ref[:, at] - xm_ref[:, at].astype(F32) * dx_ref[:, at]
        dg = jnp.sum(e.reshape(heads, HD, L), axis=1)
        hi, mid, lo = split3(dg)
        da = nn(hi, suffix) + nn(mid, suffix) + nn(lo, suffix) + later
        later = da[:, 0:1]
        da_ref[:, at] = da.astype(BF16)


def col_pair_kernel(recv_ref, after_ref, hop_ref, a_ref, xt_ref, wt_ref, scr, *, blocks, heads):
    scr[...] = recv_ref[...].astype(F32)
    halves = heads // 2
    per = 2 * halves + 1
    tri = upper(BF16)
    i0 = lax.broadcasted_iota(jnp.int32, (L, L), 0)
    i1 = lax.broadcasted_iota(jnp.int32, (L, L), 1)
    later = i0 <= i1
    gcol = tn(tri, scr[:, per * blocks, :].astype(BF16))
    grow = gcol.T
    for k in range(blocks):
        for r in range(halves):
            xt_ref[k, :, pl.ds(r * L, L)] = scr[:, per * k + r, :].astype(BF16)
            wt_ref[k, :, pl.ds(r * L, L)] = scr[:, per * k + halves + r, :].astype(BF16)
        uvt = scr[:, per * k + 2 * halves, :]
        uv = uvt.T.astype(BF16)
        u, v = uv[:HD], uv[HD:]
        s = nn(uvt[:, :HD].astype(BF16), v)
        q = None
        for h in range(heads):
            ch = pl.ds(h * HD, HD)
            c = heads * k + h
            d = jnp.exp(jnp.minimum(grow[c : c + 1, :] - gcol[:, c : c + 1], 0.0))
            d = jnp.where(later, d, 0.0)
            m = nt(xt_ref[k, :, ch], wt_ref[k, :, ch])
            dm = d * m
            q = dm if q is None else q + dm
            a_ref[c] = (d * s).astype(BF16)
        qb = q.astype(BF16)
        du = nt(v, qb).astype(BF16)
        dv = nn(u, qb).astype(BF16)
        quarter = HD // 4
        for p in range(4):
            hop_ref[p, pl.ds(2 * quarter * k, quarter), :] = du[quarter * p : quarter * (p + 1)]
            hop_ref[p, pl.ds(2 * quarter * k + quarter, quarter), :] = dv[quarter * p : quarter * (p + 1)]


def col_value_kernel(a_ref, xt_ref, wt_ref, ret_ref, da_ref, y_ref, dx_ref, *, blocks, heads):
    i0 = lax.broadcasted_iota(jnp.int32, (L, L), 0)
    i1 = lax.broadcasted_iota(jnp.int32, (L, L), 1)
    suffix = (i0 >= i1).astype(BF16)
    rows = da_ref.shape[0]
    width = heads * HD
    c0 = lax.broadcasted_iota(jnp.int32, (rows, width), 0)
    c1 = lax.broadcasted_iota(jnp.int32, (rows, width), 1)
    dg = jnp.zeros((rows, L), F32)
    for k in range(blocks):
        for h in range(heads):
            ch = pl.ds(h * HD, HD)
            a = a_ref[heads * k + h]
            dx_ref[:, ch] = nn(a, wt_ref[k, :, ch])
            y_ref[:, ch] = tn(a, xt_ref[k, :, ch])
        dx = dx_ref[...]
        for r in range(heads // 2):
            ret_ref[:, (heads // 2) * k + r, :] = dx[:, r * L : (r + 1) * L]
        e = wt_ref[k].astype(F32) * y_ref[...] - xt_ref[k].astype(F32) * dx
        start = (c0 - heads * k) * HD
        seg = ((c1 >= start) & (c1 < start + HD)).astype(BF16)
        for part in split3(e):
            dg += nt(seg, part)
    hi, mid, lo = split3(dg)
    da_ref[...] = nn(hi, suffix) + nn(mid, suffix) + nn(lo, suffix)


def pack_kernel(hop_ref, ret_ref, da_ref, out_ref, scr, *, used):
    total = hop_ref[0].astype(F32)
    for p in range(1, 4):
        total += hop_ref[p].astype(F32)
    rows = total.shape[0] + da_ref.shape[0]
    small = [total, da_ref[...], jnp.zeros((L - rows, L), F32)]
    scr[...] = ret_ref[...]
    scr[:, used, :] = jnp.concatenate(small, axis=0).T
    scr[:, used + 1, :] = jnp.zeros((L, L), F32)
    out_ref[...] = scr[...].astype(BF16)


def final_kernel(back_ref, dx_ref, tis_ref, r0_ref, r1_ref, r2_ref, r3_ref, gx_ref, iu_ref, iv_ref, cu_ref, cv_ref, da_ref, scr, *, heads):
    n = dx_ref.shape[1]
    blocks = n // L
    halves = heads // 2
    keep = keep_of(tis_ref[...], n)
    scr[...] = back_ref[...].astype(F32)
    for k in range(blocks):
        at = pl.ds(k * L, L)
        for r in range(halves):
            ch = pl.ds(r * L, L)
            both = dx_ref[ch, at] + scr[:, halves * k + r, :].T
            gx_ref[ch, at] = (both * keep[:, k * L : (k + 1) * L]).astype(BF16)
    small = scr[:, halves * blocks, :].T
    quarter = cu_ref.shape[0]
    for k in range(blocks):
        at = pl.ds(k * L, L)
        o = 2 * quarter * k
        cu_ref[:, at] = small[o : o + quarter].astype(BF16)
        cv_ref[:, at] = small[o + quarter : o + 2 * quarter].astype(BF16)
        o = 2 * quarter * blocks + heads * k
        da_ref[:, at] = small[o : o + heads].astype(BF16)
    row = r0_ref[...] + r1_ref[...].astype(F32) + r2_ref[...].astype(F32) + r3_ref[...].astype(F32)
    iu_ref[...] = row[:quarter].astype(BF16)
    iv_ref[...] = row[quarter:].astype(BF16)


def call(kernel, outs, scratch, flops, moved, name, in_specs=None):
    more = {} if in_specs is None else {"in_specs": in_specs}
    return pl.pallas_call(
        kernel,
        **more,
        out_shape=[jax.ShapeDtypeStruct(s, d) for s, d in outs],
        scratch_shapes=[pltpu.VMEM(s, F32) for s in scratch],
        compiler_params=pltpu.CompilerParams(vmem_limit_bytes=32 * 2**20),
        cost_estimate=pl.CostEstimate(flops=flops, bytes_accessed=moved, transcendentals=0),
        name=name,
    )


def body(features, cotangent, inject_row, readout_row, inject_col, readout_col, decay_row, decay_col, tissue):
    heads = decay_row.shape[0]
    chan, _, n = features.shape
    nstate = inject_row.shape[0]
    blocks = n // L
    flat = lambda x: x.reshape(x.shape[0], n)
    x, w = flat(features), flat(cotangent)
    per = 2 * chan // L + 1
    rows_out = per * blocks + 1
    send, xm, wm, wt = call(
        prep_kernel,
        [((L, rows_out, L), BF16), ((chan, n), BF16), ((chan, n), BF16), ((n, chan), BF16)],
        [(L, rows_out, L)],
        10**7, 10**6, "pack_rows",
    )(x, w, flat(inject_col), flat(readout_col), flat(decay_col), tissue)
    recv = lax.all_to_all(send, "rows", split_axis=0, concat_axis=0, tiled=True)
    share = (nstate // 2, n)
    dx_row, mine, *theirs, da_row = call(
        row_kernel,
        [((chan, n), F32), (share, F32), (share, BF16), (share, BF16), (share, BF16), ((heads, n), BF16)],
        [(chan, n), (2 * nstate, n)],
        4 * 10**9, 10**6, "row_scan",
    )(xm, wm, wt, flat(inject_row), flat(readout_row), flat(decay_row))
    shares = [
        lax.ppermute(part, "heads", [(i, (i + shift) % 4) for i in range(4)]) for shift, part in enumerate(theirs, 1)
    ]
    sizes = dict(blocks=blocks, heads=heads)
    hop, weights, xt, wtc = call(
        partial(col_pair_kernel, **sizes),
        [((4, nstate // 2 * blocks, L), BF16), ((blocks * heads, L, L), BF16), ((blocks, L, chan), BF16), ((blocks, L, chan), BF16)],
        [(L, rows_out, L)],
        10**9, 10**6, "col_pairs",
        [pl.BlockSpec(memory_space=pltpu.VMEM), pl.BlockSpec(memory_space=pl.ANY)],
    )(recv, da_row)
    hopped = lax.all_to_all(hop, "heads", split_axis=0, concat_axis=0, tiled=True)
    used = blocks * heads // 2
    ret, da_col = call(
        partial(col_value_kernel, **sizes),
        [((L, used + 2, L), F32), ((16, L), F32)],
        [(L, chan), (L, chan)],
        2 * 10**9, 10**6, "col_values",
    )(weights, xt, wtc)
    (packed,) = call(
        partial(pack_kernel, used=used), [((L, used + 2, L), BF16)], [(L, used + 2, L)], 10**7, 10**6, "pack_cols"
    )(hopped, ret, da_col)
    back = lax.all_to_all(packed, "rows", split_axis=0, concat_axis=0, tiled=True)
    quarter = nstate // 4
    gx, iu, iv, cu, cv, da = call(
        partial(final_kernel, heads=heads),
        [((chan, n), BF16)] + [((quarter, n), BF16)] * 4 + [((heads, n), BF16)],
        [(L, used + 2, L)],
        10**7, 10**6, "join",
    )(back, dx_row, tissue, mine, *shares)
    wide = lambda x: x.reshape(x.shape[0], 1, n)
    return wide(gx), wide(iu), wide(iv), wide(cu), wide(cv), wide(da_row), wide(da)


def solution(mesh):
    split = P("heads", "rows", None)
    shared = P(None, "rows", None)
    in_specs = (split, split, shared, shared, shared, shared, split, split, P("rows", None))
    return jax.shard_map(body, mesh=mesh, in_specs=in_specs, out_specs=(split,) * 7, check_vma=False)
```

```python
from functools import partial

import jax
import jax.numpy as jnp
from jax import lax
from jax.experimental import pallas as pl
from jax.experimental.pallas import tpu as pltpu
from jax.sharding import PartitionSpec as P

TILE = 16
L = 128
HD = 64
F32, BF16 = jnp.float32, jnp.bfloat16


def nn(a, b):
    return lax.dot_general(a, b, (((1,), (0,)), ((), ())), preferred_element_type=F32)


def nt(a, b):
    return lax.dot_general(a, b, (((1,), (1,)), ((), ())), preferred_element_type=F32)


def tn(a, b):
    return lax.dot_general(a, b, (((0,), (0,)), ((), ())), preferred_element_type=F32)


def upper(dtype):
    i = lax.broadcasted_iota(jnp.int32, (L, L), 0)
    j = lax.broadcasted_iota(jnp.int32, (L, L), 1)
    return (i <= j).astype(dtype)


def split3(x):
    hi = x.astype(BF16)
    r = x - hi.astype(F32)
    mid = r.astype(BF16)
    return hi, mid, (r - mid.astype(F32)).astype(BF16)


def keep_of(tissue, n):
    tiles = tissue.shape[1]
    t = lax.broadcasted_iota(jnp.int32, (tiles, n), 0) * TILE
    j = lax.broadcasted_iota(jnp.int32, (tiles, n), 1)
    spread = ((j >= t) & (j < t + TILE)).astype(F32)
    rows = jnp.broadcast_to(tissue.astype(F32), (8, tiles))
    return nn(rows, spread)[0:1]


def prep_kernel(x_any, w_any, u_any, v_any, a_any, tis_any, send_any, x_ref, w_ref, u_ref, v_ref, a_ref, tis_ref, send_ref, scr, sems, out_sems):
    n = x_ref.shape[1]
    blocks = n // L
    halves = x_ref.shape[0] // L
    per = 2 * halves + 1
    heads = a_ref.shape[0]
    pairs = [(tis_any, tis_ref), (u_any, u_ref), (v_any, v_ref), (a_any, a_ref)]
    for whole, mine in ((x_any, x_ref), (w_any, w_ref)):
        pairs += [(whole.at[pl.ds(r * L, L)], mine.at[pl.ds(r * L, L)]) for r in range(halves)]
    copies = [pltpu.make_async_copy(src, dst, sems.at[i]) for i, (src, dst) in enumerate(pairs)]
    for copy in copies:
        copy.start()
    for copy in copies[:4]:
        copy.wait()
    keep = keep_of(tis_ref[...], n)
    for k in range(blocks):
        at = pl.ds(k * L, L)
        uv = jnp.concatenate([u_ref[:, at].astype(F32), v_ref[:, at].astype(F32)], axis=0)
        scr[:, per * k + 2 * halves, :] = uv.T
    a = [a_ref[:, pl.ds(k * L, L)].astype(F32) for k in range(blocks)]
    a.append(jnp.zeros((L - heads * blocks, L), F32))
    scr[:, per * blocks, :] = jnp.concatenate(a, axis=0).T
    for o, ref in ((0, x_ref), (halves, w_ref)):
        for r in range(halves):
            copies[4 + o + r].wait()
            for k in range(blocks):
                at = pl.ds(k * L, L)
                part = ref[pl.ds(r * L, L), at].astype(F32) * keep[:, k * L : (k + 1) * L]
                scr[:, per * k + o + r, :] = part.T
    send_out(scr, send_ref, send_any, out_sems)


def send_out(src, mid, dst, sems):
    pieces = sems.shape[0]
    size = src.shape[0] // pieces
    copies = []
    for i in range(pieces):
        at = pl.ds(i * size, size)
        mid[at] = src[at].astype(mid.dtype)
        copies.append(pltpu.make_async_copy(mid.at[at], dst.at[at], sems.at[i]))
        copies[-1].start()
    for copy in copies:
        copy.wait()


def row_kernel(x_ref, w_ref, tis_ref, u_ref, v_ref, a_ref, dx_ref, d0_ref, d1_ref, d2_ref, d3_ref, da_ref, y_ref, duv_ref, xm_ref, wm_ref, wt_ref):
    n = x_ref.shape[1]
    keep = keep_of(tis_ref[...], n).astype(BF16)
    xm_ref[...] = x_ref[...] * keep
    wm_ref[...] = w_ref[...] * keep
    for b in range(n // L):
        for r in range(x_ref.shape[0] // L):
            wt_ref[pl.ds(b * L, L), pl.ds(r * L, L)] = wm_ref[pl.ds(r * L, L), pl.ds(b * L, L)].astype(F32).T.astype(BF16)
    blocks = n // L
    heads = a_ref.shape[0]
    nstate = u_ref.shape[0]
    tri = upper(BF16)
    le = upper(F32)
    carry = jnp.zeros((heads, 1), F32)
    grow, gcol = [], []
    for b in range(blocks):
        g = nn(a_ref[:, pl.ds(b * L, L)], tri) + carry
        carry = g[:, L - 1 : L]
        grow.append(g)
        gcol.append(jnp.concatenate([g, jnp.zeros((8 - heads, L), F32)], axis=0).T)
    vt = [v_ref[:, pl.ds(b * L, L)].astype(F32).T.astype(BF16) for b in range(blocks)]
    i0 = lax.broadcasted_iota(jnp.int32, (L, L), 0)
    i1 = lax.broadcasted_iota(jnp.int32, (L, L), 1)
    lower = i1 <= i0
    dv = [None] * blocks
    du = [None] * blocks
    for j in range(blocks):
        sj = pl.ds(j * L, L)
        dxs = [None] * heads
        for i in range(j, blocks):
            ti = pl.ds(i * L, L)
            s = nn(vt[i], u_ref[:, sj])
            q = None
            for h in range(heads):
                ch = pl.ds(h * HD, HD)
                d = jnp.exp(jnp.minimum(gcol[i][:, h : h + 1] - grow[j][h : h + 1, :], 0.0))
                if i == j:
                    d = jnp.where(lower, d, 0.0)
                m = nn(wt_ref[ti, ch], xm_ref[ch, sj])
                dm = d * m
                q = dm if q is None else q + dm
                a = (d * s).astype(BF16)
                part = nn(wm_ref[ch, ti], a)
                dxs[h] = part if dxs[h] is None else dxs[h] + part
                y = nt(xm_ref[ch, sj], a)
                if j == 0:
                    y_ref[ch, ti] = y
                else:
                    y_ref[ch, ti] += y
            qb = q.astype(BF16)
            pu = nn(v_ref[:, ti], qb)
            pv = nt(u_ref[:, sj], qb)
            du[j] = pu if du[j] is None else du[j] + pu
            dv[i] = pv if dv[i] is None else dv[i] + pv
        for h in range(heads):
            dx_ref[pl.ds(h * HD, HD), sj] = dxs[h]
    quarter = nstate // 4
    for b in range(blocks):
        at = pl.ds(b * L, L)
        for k in range(4):
            duv_ref[pl.ds(2 * quarter * k, quarter), at] = du[b][quarter * k : quarter * (k + 1)]
            duv_ref[pl.ds(2 * quarter * k + quarter, quarter), at] = dv[b][quarter * k : quarter * (k + 1)]
    me = lax.axis_index("heads")
    for shift, ref in enumerate((d0_ref, d1_ref, d2_ref, d3_ref)):
        part = lax.rem(me + shift, 4) * (2 * quarter)
        ref[...] = duv_ref[pl.ds(pl.multiple_of(part, 2 * quarter), 2 * quarter), :].astype(ref.dtype)
    suffix = (i0 >= i1).astype(BF16)
    later = jnp.zeros((heads, 1), F32)
    for b in reversed(range(blocks)):
        at = pl.ds(b * L, L)
        e = wm_ref[:, at].astype(F32) * y_ref[:, at] - xm_ref[:, at].astype(F32) * dx_ref[:, at]
        dg = jnp.sum(e.reshape(heads, HD, L), axis=1)
        hi, mid, lo = split3(dg)
        da = nn(hi, suffix) + nn(mid, suffix) + nn(lo, suffix) + later
        later = da[:, 0:1]
        da_ref[:, at] = da.astype(BF16)


def col_pair_kernel(recv_ref, after0_ref, after1_ref, hop_any, a_ref, xt_ref, wt_ref, scr, d_ref, hop_ref, sems, *, blocks, heads):
    scr[...] = recv_ref[...].astype(F32)
    halves = heads // 2
    per = 2 * halves + 1
    tri = upper(BF16)
    i0 = lax.broadcasted_iota(jnp.int32, (L, L), 0)
    i1 = lax.broadcasted_iota(jnp.int32, (L, L), 1)
    later = i0 <= i1
    gcol = tn(tri, scr[:, per * blocks, :].astype(BF16))
    grow = gcol.T
    quarter = HD // 4
    copies = []
    for k in range(blocks):
        for r in range(halves):
            xt_ref[k, :, pl.ds(r * L, L)] = scr[:, per * k + r, :].astype(BF16)
            wt_ref[k, :, pl.ds(r * L, L)] = scr[:, per * k + halves + r, :].astype(BF16)
        uv = scr[:, per * k + 2 * halves, :].T.astype(BF16)
        u, v = uv[:HD], uv[HD:]
        q = None
        for h in range(heads):
            ch = pl.ds(h * HD, HD)
            c = heads * k + h
            d = jnp.exp(jnp.minimum(grow[c : c + 1, :] - gcol[:, c : c + 1], 0.0))
            d = jnp.where(later, d, 0.0)
            d_ref[c] = d
            dm = d * nt(xt_ref[k, :, ch], wt_ref[k, :, ch])
            q = dm if q is None else q + dm
        qb = q.astype(BF16)
        du = nt(v, qb).astype(BF16)
        dv = nn(u, qb).astype(BF16)
        at = pl.ds(2 * quarter * k, 2 * quarter)
        for p in range(4):
            hop_ref[p, pl.ds(2 * quarter * k, quarter), :] = du[quarter * p : quarter * (p + 1)]
            hop_ref[p, pl.ds(2 * quarter * k + quarter, quarter), :] = dv[quarter * p : quarter * (p + 1)]
        copies.append(pltpu.make_async_copy(hop_ref.at[:, at], hop_any.at[:, at], sems.at[k]))
        copies[-1].start()
    for k in range(blocks):
        uvt = scr[:, per * k + 2 * halves, :]
        s = nn(uvt[:, :HD].astype(BF16), uvt.T[HD:].astype(BF16))
        for h in range(heads):
            a_ref[heads * k + h] = (d_ref[heads * k + h] * s).astype(BF16)
    for copy in copies:
        copy.wait()


def col_value_kernel(a_ref, xt_ref, wt_ref, ret_ref, da_ref, y_ref, dx_ref, *, blocks, heads):
    i0 = lax.broadcasted_iota(jnp.int32, (L, L), 0)
    i1 = lax.broadcasted_iota(jnp.int32, (L, L), 1)
    suffix = (i0 >= i1).astype(BF16)
    rows = da_ref.shape[0]
    width = heads * HD
    c0 = lax.broadcasted_iota(jnp.int32, (rows, width), 0)
    c1 = lax.broadcasted_iota(jnp.int32, (rows, width), 1)
    dg = jnp.zeros((rows, L), F32)
    for k in range(blocks):
        for h in range(heads):
            ch = pl.ds(h * HD, HD)
            a = a_ref[heads * k + h]
            dx_ref[:, ch] = nn(a, wt_ref[k, :, ch])
            y_ref[:, ch] = tn(a, xt_ref[k, :, ch])
        dx = dx_ref[...]
        for r in range(heads // 2):
            ret_ref[:, (heads // 2) * k + r, :] = dx[:, r * L : (r + 1) * L]
        e = wt_ref[k].astype(F32) * y_ref[...] - xt_ref[k].astype(F32) * dx
        start = (c0 - heads * k) * HD
        seg = ((c1 >= start) & (c1 < start + HD)).astype(BF16)
        for part in split3(e):
            dg += nt(seg, part)
    hi, mid, lo = split3(dg)
    da_ref[...] = nn(hi, suffix) + nn(mid, suffix) + nn(lo, suffix)


def pack_kernel(hop_ref, ret_ref, da_ref, out_any, scr, out_ref, sems, *, used):
    total = hop_ref[0].astype(F32)
    for p in range(1, 4):
        total += hop_ref[p].astype(F32)
    rows = total.shape[0] + da_ref.shape[0]
    small = [total, da_ref[...], jnp.zeros((L - rows, L), F32)]
    scr[...] = ret_ref[...]
    scr[:, used, :] = jnp.concatenate(small, axis=0).T
    scr[:, used + 1, :] = jnp.zeros((L, L), F32)
    send_out(scr, out_ref, out_any, sems)


def final_kernel(back_ref, dx_ref, tis_ref, r0_ref, r1_ref, r2_ref, r3_ref, gx_ref, iu_ref, iv_ref, cu_ref, cv_ref, da_ref, scr, *, heads):
    n = dx_ref.shape[1]
    blocks = n // L
    halves = heads // 2
    keep = keep_of(tis_ref[...], n)
    scr[...] = back_ref[...].astype(F32)
    for k in range(blocks):
        at = pl.ds(k * L, L)
        for r in range(halves):
            ch = pl.ds(r * L, L)
            both = dx_ref[ch, at] + scr[:, halves * k + r, :].T
            gx_ref[ch, at] = (both * keep[:, k * L : (k + 1) * L]).astype(BF16)
    small = scr[:, halves * blocks, :].T
    quarter = cu_ref.shape[0]
    for k in range(blocks):
        at = pl.ds(k * L, L)
        o = 2 * quarter * k
        cu_ref[:, at] = small[o : o + quarter].astype(BF16)
        cv_ref[:, at] = small[o + quarter : o + 2 * quarter].astype(BF16)
        o = 2 * quarter * blocks + heads * k
        da_ref[:, at] = small[o : o + heads].astype(BF16)
    row = r0_ref[...] + r1_ref[...].astype(F32) + r2_ref[...].astype(F32) + r3_ref[...].astype(F32)
    iu_ref[...] = row[:quarter].astype(BF16)
    iv_ref[...] = row[quarter:].astype(BF16)


def call(kernel, outs, scratch, flops, name, limit=32, ins=None):
    place = lambda far: pl.BlockSpec(memory_space=pl.ANY if far else pltpu.VMEM)
    more = {} if ins is None else {"in_specs": [place(far) for far in ins]}
    return pl.pallas_call(
        kernel,
        **more,
        out_shape=[jax.ShapeDtypeStruct(o[0], o[1]) for o in outs],
        out_specs=[place(len(o) > 2) for o in outs],
        scratch_shapes=scratch,
        compiler_params=pltpu.CompilerParams(vmem_limit_bytes=limit * 2**20),
        cost_estimate=pl.CostEstimate(flops=flops, bytes_accessed=10**6, transcendentals=0),
        name=name,
    )


def body(features, cotangent, inject_row, readout_row, inject_col, readout_col, decay_row, decay_col, tissue):
    heads = decay_row.shape[0]
    chan, _, n = features.shape
    nstate = inject_row.shape[0]
    quarter = nstate // 4
    blocks = n // L
    flat = lambda x: x.reshape(x.shape[0], n)
    vm, dma = pltpu.VMEM, pltpu.SemaphoreType.DMA
    x, w = flat(features), flat(cotangent)
    per = 2 * chan // L + 1
    rows_out = per * blocks + 1
    tile = (L, rows_out, L)
    (send,) = call(
        prep_kernel,
        [(tile, BF16, "far")],
        [
            vm((chan, n), BF16), vm((chan, n), BF16), vm((nstate, n), BF16), vm((nstate, n), BF16),
            vm((heads, n), BF16), vm(tissue.shape, jnp.int32), vm(tile, BF16), vm(tile, F32),
            dma((4 + 2 * chan // L,)), dma((8,)),
        ],
        10**7, "pack_rows", 60, [True] * 6,
    )(x, w, flat(inject_col), flat(readout_col), flat(decay_col), tissue)
    recv = lax.all_to_all(send, "rows", split_axis=0, concat_axis=0, tiled=True)
    share = (2 * quarter, n)
    dx_row, mine, *theirs, da_row = call(
        row_kernel,
        [((chan, n), F32), (share, F32), (share, BF16), (share, BF16), (share, BF16), ((heads, n), BF16)],
        [vm((chan, n), F32), vm((2 * nstate, n), F32), vm((chan, n), BF16), vm((chan, n), BF16), vm((n, chan), BF16)],
        4 * 10**9, "row_scan",
    )(x, w, tissue, flat(inject_row), flat(readout_row), flat(decay_row))
    shares = [
        lax.ppermute(part, "heads", [(i, (i + shift) % 4) for i in range(4)]) for shift, part in enumerate(theirs, 1)
    ]
    sizes = dict(blocks=blocks, heads=heads)
    hop_shape = (4, 2 * quarter * blocks, L)
    per_col = (blocks, L, chan)
    hop, weights, xt, wtc = call(
        partial(col_pair_kernel, **sizes),
        [(hop_shape, BF16, "far"), ((blocks * heads, L, L), BF16), (per_col, BF16), (per_col, BF16)],
        [vm(tile, F32), vm((blocks * heads, L, L), F32), vm(hop_shape, BF16), dma((blocks,))],
        10**9, "col_pairs",
    )(recv, shares[0], shares[2])
    hopped = lax.all_to_all(hop, "heads", split_axis=0, concat_axis=0, tiled=True)
    used = blocks * heads // 2
    back_tile = (L, used + 2, L)
    ret, da_col = call(
        partial(col_value_kernel, **sizes),
        [(back_tile, F32), ((16, L), F32)],
        [vm((L, chan), F32), vm((L, chan), F32)],
        2 * 10**9, "col_values",
    )(weights, xt, wtc)
    (packed,) = call(
        partial(pack_kernel, used=used),
        [(back_tile, BF16, "far")],
        [vm(back_tile, F32), vm(back_tile, BF16), dma((4,))],
        10**7, "pack_cols",
    )(hopped, ret, da_col)
    back = lax.all_to_all(packed, "rows", split_axis=0, concat_axis=0, tiled=True)
    gx, iu, iv, cu, cv, da = call(
        partial(final_kernel, heads=heads),
        [((chan, n), BF16)] + [((quarter, n), BF16)] * 4 + [((heads, n), BF16)],
        [vm(back_tile, F32)],
        10**7, "join",
    )(back, dx_row, tissue, mine, *shares)
    wide = lambda x: x.reshape(x.shape[0], 1, n)
    return wide(gx), wide(iu), wide(iv), wide(cu), wide(cv), wide(da_row), wide(da)


def solution(mesh):
    split = P("heads", "rows", None)
    shared = P(None, "rows", None)
    in_specs = (split, split, shared, shared, shared, shared, split, split, P("rows", None))
    return jax.shard_map(body, mesh=mesh, in_specs=in_specs, out_specs=(split,) * 7, check_vma=False)
```

```python
from functools import partial

import jax
import jax.numpy as jnp
from jax import lax
from jax.experimental import pallas as pl
from jax.experimental.pallas import tpu as pltpu
from jax.sharding import PartitionSpec as P

TILE = 16
L = 128
HD = 64
F32, BF16 = jnp.float32, jnp.bfloat16


def nn(a, b):
    return lax.dot_general(a, b, (((1,), (0,)), ((), ())), preferred_element_type=F32)


def nt(a, b):
    return lax.dot_general(a, b, (((1,), (1,)), ((), ())), preferred_element_type=F32)


def tn(a, b):
    return lax.dot_general(a, b, (((0,), (0,)), ((), ())), preferred_element_type=F32)


def upper(dtype):
    i = lax.broadcasted_iota(jnp.int32, (L, L), 0)
    j = lax.broadcasted_iota(jnp.int32, (L, L), 1)
    return (i <= j).astype(dtype)


def head_lanes():
    lane = lax.broadcasted_iota(jnp.int32, (1, L), 1)
    return (lane < HD).astype(BF16), (lane >= HD).astype(BF16)


def split3(x):
    hi = x.astype(BF16)
    r = x - hi.astype(F32)
    mid = r.astype(BF16)
    return hi, mid, (r - mid.astype(F32)).astype(BF16)


def keep_of(tissue, n):
    tiles = tissue.shape[1]
    t = lax.broadcasted_iota(jnp.int32, (tiles, n), 0) * TILE
    j = lax.broadcasted_iota(jnp.int32, (tiles, n), 1)
    spread = ((j >= t) & (j < t + TILE)).astype(F32)
    rows = jnp.broadcast_to(tissue.astype(F32), (8, tiles))
    return nn(rows, spread)[0:1]


def prep_kernel(x_any, w_any, u_any, v_any, a_any, tis_any, send_any, x_ref, w_ref, u_ref, v_ref, a_ref, tis_ref, send_ref, scr, sems, out_sems):
    n = x_ref.shape[1]
    blocks = n // L
    halves = x_ref.shape[0] // L
    per = 2 * halves + 1
    heads = a_ref.shape[0]
    pairs = [(tis_any, tis_ref), (u_any, u_ref), (v_any, v_ref), (a_any, a_ref)]
    for whole, mine in ((x_any, x_ref), (w_any, w_ref)):
        pairs += [(whole.at[pl.ds(r * L, L)], mine.at[pl.ds(r * L, L)]) for r in range(halves)]
    copies = [pltpu.make_async_copy(src, dst, sems.at[i]) for i, (src, dst) in enumerate(pairs)]
    for copy in copies:
        copy.start()
    for copy in copies[:4]:
        copy.wait()
    keep = keep_of(tis_ref[...], n).astype(BF16)
    for k in range(blocks):
        at = pl.ds(k * L, L)
        uv = jnp.concatenate([u_ref[:, at].astype(F32), v_ref[:, at].astype(F32)], axis=0)
        scr[:, per * k + 2 * halves, :] = uv.T
    a = [a_ref[:, pl.ds(k * L, L)].astype(F32) for k in range(blocks)]
    a.append(jnp.zeros((L - heads * blocks, L), F32))
    scr[:, per * blocks, :] = jnp.concatenate(a, axis=0).T
    for o, ref in ((0, x_ref), (halves, w_ref)):
        for r in range(halves):
            copies[4 + o + r].wait()
            for k in range(blocks):
                at = pl.ds(k * L, L)
                part = ref[pl.ds(r * L, L), at] * keep[:, k * L : (k + 1) * L]
                scr[:, per * k + o + r, :] = part.T.astype(F32)
    send_out(scr, send_ref, send_any, out_sems)


def send_out(src, mid, dst, sems):
    pieces = sems.shape[0]
    size = src.shape[0] // pieces
    copies = []
    for i in range(pieces):
        at = pl.ds(i * size, size)
        mid[at] = src[at].astype(mid.dtype)
        copies.append(pltpu.make_async_copy(mid.at[at], dst.at[at], sems.at[i]))
        copies[-1].start()
    for copy in copies:
        copy.wait()


def row_kernel(x_ref, w_ref, tis_ref, u_ref, v_ref, a_ref, dx_ref, own_ref, give_ref, da_ref, y_ref, duv_ref, xm_ref, wm_ref, wt_ref):
    n = x_ref.shape[1]
    keep = keep_of(tis_ref[...], n).astype(BF16)
    xm_ref[...] = x_ref[...] * keep
    wm_ref[...] = w_ref[...] * keep
    for b in range(n // L):
        for r in range(x_ref.shape[0] // L):
            wt_ref[pl.ds(b * L, L), pl.ds(r * L, L)] = wm_ref[pl.ds(r * L, L), pl.ds(b * L, L)].astype(F32).T.astype(BF16)
    blocks = n // L
    heads = a_ref.shape[0]
    nstate = u_ref.shape[0]
    tri = upper(BF16)
    le = upper(F32)
    carry = jnp.zeros((heads, 1), F32)
    grow, gcol = [], []
    for b in range(blocks):
        g = nn(a_ref[:, pl.ds(b * L, L)], tri) + carry
        carry = g[:, L - 1 : L]
        grow.append(g)
        gcol.append(jnp.concatenate([g, jnp.zeros((8 - heads, L), F32)], axis=0).T)
    vt = [v_ref[:, pl.ds(b * L, L)].astype(F32).T.astype(BF16) for b in range(blocks)]
    i0 = lax.broadcasted_iota(jnp.int32, (L, L), 0)
    i1 = lax.broadcasted_iota(jnp.int32, (L, L), 1)
    lower = i1 <= i0
    dv = [None] * blocks
    du = [None] * blocks
    for j in range(blocks):
        sj = pl.ds(j * L, L)
        dxs = [None] * heads
        for i in range(j, blocks):
            ti = pl.ds(i * L, L)
            s = nn(vt[i], u_ref[:, sj])
            q = None
            for h in range(heads):
                ch = pl.ds(h * HD, HD)
                d = jnp.exp(jnp.minimum(gcol[i][:, h : h + 1] - grow[j][h : h + 1, :], 0.0))
                if i == j:
                    d = jnp.where(lower, d, 0.0)
                m = nn(wt_ref[ti, ch], xm_ref[ch, sj])
                dm = d * m
                q = dm if q is None else q + dm
                a = (d * s).astype(BF16)
                part = nn(wm_ref[ch, ti], a)
                dxs[h] = part if dxs[h] is None else dxs[h] + part
                y = nt(xm_ref[ch, sj], a)
                if j == 0:
                    y_ref[ch, ti] = y
                else:
                    y_ref[ch, ti] += y
            qb = q.astype(BF16)
            pu = nn(v_ref[:, ti], qb)
            pv = nt(u_ref[:, sj], qb)
            du[j] = pu if du[j] is None else du[j] + pu
            dv[i] = pv if dv[i] is None else dv[i] + pv
        for h in range(heads):
            dx_ref[pl.ds(h * HD, HD), sj] = dxs[h]
    quarter = nstate // 4
    for b in range(blocks):
        at = pl.ds(b * L, L)
        for k in range(4):
            duv_ref[pl.ds(2 * quarter * k, quarter), at] = du[b][quarter * k : quarter * (k + 1)]
            duv_ref[pl.ds(2 * quarter * k + quarter, quarter), at] = dv[b][quarter * k : quarter * (k + 1)]
    me = lax.axis_index("heads")
    part = 2 * quarter
    for slot, near in enumerate((me, lax.rem(me + 2, 4))):
        far = near + 1 - 2 * lax.rem(near, 2)
        to = pl.ds(slot * part, part)
        own_ref[to, :] = duv_ref[pl.ds(pl.multiple_of(near * part, part), part), :]
        give_ref[to, :] = duv_ref[pl.ds(pl.multiple_of(far * part, part), part), :].astype(give_ref.dtype)
    suffix = (i0 >= i1).astype(BF16)
    later = jnp.zeros((heads, 1), F32)
    for b in reversed(range(blocks)):
        at = pl.ds(b * L, L)
        e = wm_ref[:, at].astype(F32) * y_ref[:, at] - xm_ref[:, at].astype(F32) * dx_ref[:, at]
        dg = jnp.sum(e.reshape(heads, HD, L), axis=1)
        hi, mid, lo = split3(dg)
        da = nn(hi, suffix) + nn(mid, suffix) + nn(lo, suffix) + later
        later = da[:, 0:1]
        da_ref[:, at] = da.astype(BF16)


def col_pair_kernel(recv_ref, after_ref, hop_any, a_ref, xt_ref, wt_ref, scr, d_ref, hop_ref, sems, *, blocks, heads):
    scr[...] = recv_ref[...].astype(F32)
    halves = heads // 2
    per = 2 * halves + 1
    tri = upper(BF16)
    i0 = lax.broadcasted_iota(jnp.int32, (L, L), 0)
    i1 = lax.broadcasted_iota(jnp.int32, (L, L), 1)
    later = i0 <= i1
    half = head_lanes()
    gcol = tn(tri, scr[:, per * blocks, :].astype(BF16))
    grow = gcol.T
    quarter = HD // 4
    copies = []
    for k in range(blocks):
        for r in range(halves):
            xt_ref[k, :, pl.ds(r * L, L)] = scr[:, per * k + r, :].astype(BF16)
            wt_ref[k, :, pl.ds(r * L, L)] = scr[:, per * k + halves + r, :].astype(BF16)
        uv = scr[:, per * k + 2 * halves, :].T.astype(BF16)
        u, v = uv[:HD], uv[HD:]
        q = None
        for h in range(heads):
            c = heads * k + h
            d = jnp.exp(jnp.minimum(grow[c : c + 1, :] - gcol[:, c : c + 1], 0.0))
            d = jnp.where(later, d, 0.0)
            d_ref[c] = d
            pair = pl.ds(h // 2 * L, L)
            dm = d * nt(xt_ref[k, :, pair] * half[h % 2], wt_ref[k, :, pair])
            q = dm if q is None else q + dm
        qb = q.astype(BF16)
        du = nt(v, qb).astype(BF16)
        dv = nn(u, qb).astype(BF16)
        at = pl.ds(2 * quarter * k, 2 * quarter)
        for p in range(4):
            hop_ref[p, pl.ds(2 * quarter * k, quarter), :] = du[quarter * p : quarter * (p + 1)]
            hop_ref[p, pl.ds(2 * quarter * k + quarter, quarter), :] = dv[quarter * p : quarter * (p + 1)]
        copies.append(pltpu.make_async_copy(hop_ref.at[:, at], hop_any.at[:, at], sems.at[k]))
        copies[-1].start()
    for k in range(blocks):
        uvt = scr[:, per * k + 2 * halves, :]
        s = nn(uvt[:, :HD].astype(BF16), uvt.T[HD:].astype(BF16))
        for h in range(heads):
            a_ref[heads * k + h] = (d_ref[heads * k + h] * s).astype(BF16)
    for copy in copies:
        copy.wait()


def col_value_kernel(a_ref, xt_ref, wt_ref, own_ref, near_ref, ret_ref, da_ref, mine_ref, pass_ref, y_ref, dx_ref, *, blocks, heads):
    part = mine_ref.shape[0]
    mine_ref[...] = own_ref[:part] + near_ref[:part].astype(F32)
    pass_ref[...] = (own_ref[part:] + near_ref[part:].astype(F32)).astype(pass_ref.dtype)
    i0 = lax.broadcasted_iota(jnp.int32, (L, L), 0)
    i1 = lax.broadcasted_iota(jnp.int32, (L, L), 1)
    suffix = (i0 >= i1).astype(BF16)
    half = head_lanes()
    rows = da_ref.shape[0]
    width = heads * HD
    c0 = lax.broadcasted_iota(jnp.int32, (rows, width), 0)
    c1 = lax.broadcasted_iota(jnp.int32, (rows, width), 1)
    dg = jnp.zeros((rows, L), F32)
    for k in range(blocks):
        for r in range(heads // 2):
            pair = pl.ds(r * L, L)
            a0, a1 = a_ref[heads * k + 2 * r], a_ref[heads * k + 2 * r + 1]
            w, x = wt_ref[k, :, pair], xt_ref[k, :, pair]
            dx_ref[:, pair] = nn(jnp.concatenate([a0, a1], axis=1), jnp.concatenate([w * half[0], w * half[1]], axis=0))
            y_ref[:, pair] = tn(jnp.concatenate([a0, a1], axis=0), jnp.concatenate([x * half[0], x * half[1]], axis=0))
        dx = dx_ref[...]
        for r in range(heads // 2):
            ret_ref[:, (heads // 2) * k + r, :] = dx[:, r * L : (r + 1) * L]
        e = wt_ref[k].astype(F32) * y_ref[...] - xt_ref[k].astype(F32) * dx
        start = (c0 - heads * k) * HD
        seg = ((c1 >= start) & (c1 < start + HD)).astype(BF16)
        for part in split3(e):
            dg += nt(seg, part)
    hi, mid, lo = split3(dg)
    da_ref[...] = nn(hi, suffix) + nn(mid, suffix) + nn(lo, suffix)


def pack_kernel(hop_ref, ret_ref, da_ref, out_any, scr, out_ref, sems, *, used):
    total = hop_ref[0].astype(F32)
    for p in range(1, 4):
        total += hop_ref[p].astype(F32)
    rows = total.shape[0] + da_ref.shape[0]
    small = [total, da_ref[...], jnp.zeros((L - rows, L), F32)]
    scr[...] = ret_ref[...]
    scr[:, used, :] = jnp.concatenate(small, axis=0).T
    scr[:, used + 1, :] = jnp.zeros((L, L), F32)
    send_out(scr, out_ref, out_any, sems)


def final_kernel(back_ref, dx_ref, tis_ref, mine_ref, other_ref, gx_ref, iu_ref, iv_ref, cu_ref, cv_ref, da_ref, scr, *, heads):
    n = dx_ref.shape[1]
    blocks = n // L
    halves = heads // 2
    keep = keep_of(tis_ref[...], n)
    scr[...] = back_ref[...].astype(F32)
    for k in range(blocks):
        at = pl.ds(k * L, L)
        for r in range(halves):
            ch = pl.ds(r * L, L)
            both = dx_ref[ch, at] + scr[:, halves * k + r, :].T
            gx_ref[ch, at] = (both * keep[:, k * L : (k + 1) * L]).astype(BF16)
    small = scr[:, halves * blocks, :].T
    quarter = cu_ref.shape[0]
    for k in range(blocks):
        at = pl.ds(k * L, L)
        o = 2 * quarter * k
        cu_ref[:, at] = small[o : o + quarter].astype(BF16)
        cv_ref[:, at] = small[o + quarter : o + 2 * quarter].astype(BF16)
        o = 2 * quarter * blocks + heads * k
        da_ref[:, at] = small[o : o + heads].astype(BF16)
    row = mine_ref[...] + other_ref[...].astype(F32)
    iu_ref[...] = row[:quarter].astype(BF16)
    iv_ref[...] = row[quarter:].astype(BF16)


def call(kernel, outs, scratch, flops, name, limit=32, ins=None):
    place = lambda far: pl.BlockSpec(memory_space=pl.ANY if far else pltpu.VMEM)
    more = {} if ins is None else {"in_specs": [place(far) for far in ins]}
    return pl.pallas_call(
        kernel,
        **more,
        out_shape=[jax.ShapeDtypeStruct(o[0], o[1]) for o in outs],
        out_specs=[place(len(o) > 2) for o in outs],
        scratch_shapes=scratch,
        compiler_params=pltpu.CompilerParams(vmem_limit_bytes=limit * 2**20),
        cost_estimate=pl.CostEstimate(flops=flops, bytes_accessed=10**6, transcendentals=0),
        name=name,
    )


def body(features, cotangent, inject_row, readout_row, inject_col, readout_col, decay_row, decay_col, tissue):
    heads = decay_row.shape[0]
    chan, _, n = features.shape
    nstate = inject_row.shape[0]
    quarter = nstate // 4
    blocks = n // L
    flat = lambda x: x.reshape(x.shape[0], n)
    vm, dma = pltpu.VMEM, pltpu.SemaphoreType.DMA
    x, w = flat(features), flat(cotangent)
    per = 2 * chan // L + 1
    rows_out = per * blocks + 1
    tile = (L, rows_out, L)
    (send,) = call(
        prep_kernel,
        [(tile, BF16, "far")],
        [
            vm((chan, n), BF16), vm((chan, n), BF16), vm((nstate, n), BF16), vm((nstate, n), BF16),
            vm((heads, n), BF16), vm(tissue.shape, jnp.int32), vm(tile, BF16), vm(tile, F32),
            dma((4 + 2 * chan // L,)), dma((8,)),
        ],
        10**7, "pack_rows", 60, [True] * 6,
    )(x, w, flat(inject_col), flat(readout_col), flat(decay_col), tissue)
    recv = lax.all_to_all(send, "rows", split_axis=0, concat_axis=0, tiled=True)
    share = (2 * quarter, n)
    two = (4 * quarter, n)
    dx_row, own, give, da_row = call(
        row_kernel,
        [((chan, n), F32), (two, F32), (two, BF16), ((heads, n), BF16)],
        [vm((chan, n), F32), vm((2 * nstate, n), F32), vm((chan, n), BF16), vm((chan, n), BF16), vm((n, chan), BF16)],
        4 * 10**9, "row_scan",
    )(x, w, tissue, flat(inject_row), flat(readout_row), flat(decay_row))
    near = lax.ppermute(give, "heads", [(i, i ^ 1) for i in range(4)])
    sizes = dict(blocks=blocks, heads=heads)
    hop_shape = (4, 2 * quarter * blocks, L)
    per_col = (blocks, L, chan)
    hop, weights, xt, wtc = call(
        partial(col_pair_kernel, **sizes),
        [(hop_shape, BF16, "far"), ((blocks * heads, L, L), BF16), (per_col, BF16), (per_col, BF16)],
        [vm(tile, F32), vm((blocks * heads, L, L), F32), vm(hop_shape, BF16), dma((blocks,))],
        10**9, "col_pairs",
    )(recv, near)
    hopped = lax.all_to_all(hop, "heads", split_axis=0, concat_axis=0, tiled=True)
    used = blocks * heads // 2
    back_tile = (L, used + 2, L)
    ret, da_col, mine, give = call(
        partial(col_value_kernel, **sizes),
        [(back_tile, F32), ((16, L), F32), (share, F32), (share, BF16)],
        [vm((L, chan), F32), vm((L, chan), F32)],
        2 * 10**9, "col_values",
    )(weights, xt, wtc, own, near)
    other = lax.ppermute(give, "heads", [(i, i ^ 2) for i in range(4)])
    (packed,) = call(
        partial(pack_kernel, used=used),
        [(back_tile, BF16, "far")],
        [vm(back_tile, F32), vm(back_tile, BF16), dma((4,))],
        10**7, "pack_cols",
    )(hopped, ret, da_col)
    back = lax.all_to_all(packed, "rows", split_axis=0, concat_axis=0, tiled=True)
    gx, iu, iv, cu, cv, da = call(
        partial(final_kernel, heads=heads),
        [((chan, n), BF16)] + [((quarter, n), BF16)] * 4 + [((heads, n), BF16)],
        [vm(back_tile, F32)],
        10**7, "join",
    )(back, dx_row, tissue, mine, other)
    wide = lambda x: x.reshape(x.shape[0], 1, n)
    return wide(gx), wide(iu), wide(iv), wide(cu), wide(cv), wide(da_row), wide(da)


def solution(mesh):
    split = P("heads", "rows", None)
    shared = P(None, "rows", None)
    in_specs = (split, split, shared, shared, shared, shared, split, split, P("rows", None))
    return jax.shard_map(body, mesh=mesh, in_specs=in_specs, out_specs=(split,) * 7, check_vma=False)
```

```python
from functools import partial

import jax
import jax.numpy as jnp
from jax import lax
from jax.experimental import pallas as pl
from jax.experimental.pallas import tpu as pltpu
from jax.sharding import PartitionSpec as P

TILE = 16
L = 128
HD = 64
F32, BF16 = jnp.float32, jnp.bfloat16


def nn(a, b):
    return lax.dot_general(a, b, (((1,), (0,)), ((), ())), preferred_element_type=F32)


def nt(a, b):
    return lax.dot_general(a, b, (((1,), (1,)), ((), ())), preferred_element_type=F32)


def tn(a, b):
    return lax.dot_general(a, b, (((0,), (0,)), ((), ())), preferred_element_type=F32)


def upper(dtype):
    i = lax.broadcasted_iota(jnp.int32, (L, L), 0)
    j = lax.broadcasted_iota(jnp.int32, (L, L), 1)
    return (i <= j).astype(dtype)


def head_lanes():
    lane = lax.broadcasted_iota(jnp.int32, (1, L), 1)
    return (lane < HD).astype(BF16), (lane >= HD).astype(BF16)


def split3(x):
    hi = x.astype(BF16)
    r = x - hi.astype(F32)
    mid = r.astype(BF16)
    return hi, mid, (r - mid.astype(F32)).astype(BF16)


def keep_of(tissue, n):
    tiles = tissue.shape[1]
    t = lax.broadcasted_iota(jnp.int32, (tiles, n), 0) * TILE
    j = lax.broadcasted_iota(jnp.int32, (tiles, n), 1)
    spread = ((j >= t) & (j < t + TILE)).astype(F32)
    rows = jnp.broadcast_to(tissue.astype(F32), (8, tiles))
    return nn(rows, spread)[0:1]


def prep_kernel(x_any, w_any, u_any, v_any, a_any, tis_any, send_any, x_ref, w_ref, u_ref, v_ref, a_ref, tis_ref, send_ref, scr, sems, out_sems):
    n = x_ref.shape[1]
    blocks = n // L
    halves = x_ref.shape[0] // L
    per = 2 * halves + 1
    heads = a_ref.shape[0]
    pairs = [(tis_any, tis_ref), (u_any, u_ref), (v_any, v_ref), (a_any, a_ref)]
    for whole, mine in ((x_any, x_ref), (w_any, w_ref)):
        pairs += [(whole.at[pl.ds(r * L, L)], mine.at[pl.ds(r * L, L)]) for r in range(halves)]
    copies = [pltpu.make_async_copy(src, dst, sems.at[i]) for i, (src, dst) in enumerate(pairs)]
    for copy in copies:
        copy.start()
    for copy in copies[:4]:
        copy.wait()
    keep = keep_of(tis_ref[...], n).astype(BF16)
    for k in range(blocks):
        at = pl.ds(k * L, L)
        uv = jnp.concatenate([u_ref[:, at].astype(F32), v_ref[:, at].astype(F32)], axis=0)
        scr[:, per * k + 2 * halves, :] = uv.T
    a = [a_ref[:, pl.ds(k * L, L)].astype(F32) for k in range(blocks)]
    a.append(jnp.zeros((L - heads * blocks, L), F32))
    scr[:, per * blocks, :] = jnp.concatenate(a, axis=0).T
    for o, ref in ((0, x_ref), (halves, w_ref)):
        for r in range(halves):
            copies[4 + o + r].wait()
            for k in range(blocks):
                at = pl.ds(k * L, L)
                part = ref[pl.ds(r * L, L), at] * keep[:, k * L : (k + 1) * L]
                scr[:, per * k + o + r, :] = part.T.astype(F32)
    send_out(scr, send_ref, send_any, out_sems)


def send_out(src, mid, dst, sems):
    pieces = sems.shape[0]
    size = src.shape[0] // pieces
    copies = []
    for i in range(pieces):
        at = pl.ds(i * size, size)
        mid[at] = src[at].astype(mid.dtype)
        copies.append(pltpu.make_async_copy(mid.at[at], dst.at[at], sems.at[i]))
        copies[-1].start()
    for copy in copies:
        copy.wait()


def row_kernel(x_ref, w_ref, tis_ref, u_ref, v_ref, a_ref, dx_ref, own_ref, give_ref, da_ref, y_ref, duv_ref, xm_ref, wm_ref, wt_ref):
    n = x_ref.shape[1]
    keep = keep_of(tis_ref[...], n).astype(BF16)
    xm_ref[...] = x_ref[...] * keep
    wm_ref[...] = w_ref[...] * keep
    for b in range(n // L):
        for r in range(x_ref.shape[0] // L):
            wt_ref[pl.ds(b * L, L), pl.ds(r * L, L)] = wm_ref[pl.ds(r * L, L), pl.ds(b * L, L)].astype(F32).T.astype(BF16)
    blocks = n // L
    heads = a_ref.shape[0]
    nstate = u_ref.shape[0]
    tri = upper(BF16)
    le = upper(F32)
    carry = jnp.zeros((heads, 1), F32)
    grow, gcol = [], []
    for b in range(blocks):
        g = nn(a_ref[:, pl.ds(b * L, L)], tri) + carry
        carry = g[:, L - 1 : L]
        grow.append(g)
        gcol.append(jnp.concatenate([g, jnp.zeros((8 - heads, L), F32)], axis=0).T)
    vt = [v_ref[:, pl.ds(b * L, L)].astype(F32).T.astype(BF16) for b in range(blocks)]
    i0 = lax.broadcasted_iota(jnp.int32, (L, L), 0)
    i1 = lax.broadcasted_iota(jnp.int32, (L, L), 1)
    lower = i1 <= i0
    dv = [None] * blocks
    du = [None] * blocks
    for j in range(blocks):
        sj = pl.ds(j * L, L)
        dxs = [None] * heads
        for i in range(j, blocks):
            ti = pl.ds(i * L, L)
            s = nn(vt[i], u_ref[:, sj])
            q = None
            for h in range(heads):
                ch = pl.ds(h * HD, HD)
                d = jnp.exp(jnp.minimum(gcol[i][:, h : h + 1] - grow[j][h : h + 1, :], 0.0))
                if i == j:
                    d = jnp.where(lower, d, 0.0)
                m = nn(wt_ref[ti, ch], xm_ref[ch, sj])
                dm = d * m
                q = dm if q is None else q + dm
                a = (d * s).astype(BF16)
                part = nn(wm_ref[ch, ti], a)
                dxs[h] = part if dxs[h] is None else dxs[h] + part
                y = nt(xm_ref[ch, sj], a)
                if j == 0:
                    y_ref[ch, ti] = y
                else:
                    y_ref[ch, ti] += y
            qb = q.astype(BF16)
            pu = nn(v_ref[:, ti], qb)
            pv = nt(u_ref[:, sj], qb)
            du[j] = pu if du[j] is None else du[j] + pu
            dv[i] = pv if dv[i] is None else dv[i] + pv
        for h in range(heads):
            dx_ref[pl.ds(h * HD, HD), sj] = dxs[h]
    quarter = nstate // 4
    for b in range(blocks):
        at = pl.ds(b * L, L)
        for k in range(4):
            duv_ref[pl.ds(2 * quarter * k, quarter), at] = du[b][quarter * k : quarter * (k + 1)]
            duv_ref[pl.ds(2 * quarter * k + quarter, quarter), at] = dv[b][quarter * k : quarter * (k + 1)]
    me = lax.axis_index("heads")
    part = 2 * quarter
    for slot, near in enumerate((me, lax.rem(me + 2, 4))):
        far = near + 1 - 2 * lax.rem(near, 2)
        to = pl.ds(slot * part, part)
        own_ref[to, :] = duv_ref[pl.ds(pl.multiple_of(near * part, part), part), :]
        give_ref[to, :] = duv_ref[pl.ds(pl.multiple_of(far * part, part), part), :].astype(give_ref.dtype)
    suffix = (i0 >= i1).astype(BF16)
    later = jnp.zeros((heads, 1), F32)
    for b in reversed(range(blocks)):
        at = pl.ds(b * L, L)
        e = wm_ref[:, at].astype(F32) * y_ref[:, at] - xm_ref[:, at].astype(F32) * dx_ref[:, at]
        dg = jnp.sum(e.reshape(heads, HD, L), axis=1)
        hi, mid, lo = split3(dg)
        da = nn(hi, suffix) + nn(mid, suffix) + nn(lo, suffix) + later
        later = da[:, 0:1]
        da_ref[:, at] = da.astype(BF16)


def col_kernel(recv_ref, own_ref, near_ref, hop_ref, ret_ref, da_ref, mine_ref, pass_ref, scr, y_ref, dx_ref, *, blocks, heads):
    part = mine_ref.shape[0]
    mine_ref[...] = own_ref[:part] + near_ref[:part].astype(F32)
    pass_ref[...] = (own_ref[part:] + near_ref[part:].astype(F32)).astype(pass_ref.dtype)
    scr[...] = recv_ref[...].astype(F32)
    halves = heads // 2
    per = 2 * halves + 1
    half = head_lanes()
    i0 = lax.broadcasted_iota(jnp.int32, (L, L), 0)
    i1 = lax.broadcasted_iota(jnp.int32, (L, L), 1)
    later = i0 <= i1
    gcol = nn((i1 <= i0).astype(BF16), scr[:, per * blocks, :].astype(BF16))
    grow = gcol.T
    quarter = HD // 4
    rows = da_ref.shape[0]
    width = heads * HD
    c0 = lax.broadcasted_iota(jnp.int32, (rows, width), 0)
    c1 = lax.broadcasted_iota(jnp.int32, (rows, width), 1)
    dg = jnp.zeros((rows, L), F32)
    for k in range(blocks):
        uvt = scr[:, per * k + 2 * halves, :]
        uv = uvt.T.astype(BF16)
        u, v = uv[:HD], uv[HD:]
        s = nn(uvt[:, :HD].astype(BF16), v)
        q = None
        xs = [scr[:, per * k + r, :] for r in range(halves)]
        ws = [scr[:, per * k + halves + r, :] for r in range(halves)]
        for r in range(halves):
            pair = pl.ds(r * L, L)
            x, w = xs[r].astype(BF16), ws[r].astype(BF16)
            x_of = [x * half[0], x * half[1]]
            w_of = [w * half[0], w * half[1]]
            a = []
            for h in range(2):
                c = heads * k + 2 * r + h
                d = jnp.exp(jnp.minimum(grow[c : c + 1, :] - gcol[:, c : c + 1], 0.0))
                d = jnp.where(later, d, 0.0)
                dm = d * nt(x_of[h], w)
                q = dm if q is None else q + dm
                a.append((d * s).astype(BF16))
            dx_ref[:, pair] = nn(jnp.concatenate(a, axis=1), jnp.concatenate(w_of, axis=0))
            y_ref[:, pair] = tn(jnp.concatenate(a, axis=0), jnp.concatenate(x_of, axis=0))
        qb = q.astype(BF16)
        du = nt(v, qb).astype(BF16)
        dv = nn(u, qb).astype(BF16)
        for p in range(4):
            hop_ref[p, pl.ds(2 * quarter * k, quarter), :] = du[quarter * p : quarter * (p + 1)]
            hop_ref[p, pl.ds(2 * quarter * k + quarter, quarter), :] = dv[quarter * p : quarter * (p + 1)]
        dx = dx_ref[...]
        for r in range(halves):
            ret_ref[:, halves * k + r, :] = dx[:, r * L : (r + 1) * L]
        e = jnp.concatenate(ws, axis=1) * y_ref[...] - jnp.concatenate(xs, axis=1) * dx
        start = (c0 - heads * k) * HD
        seg = ((c1 >= start) & (c1 < start + HD)).astype(BF16)
        for term in split3(e):
            dg += nt(seg, term)
    suffix = (i0 >= i1).astype(BF16)
    hi, mid, lo = split3(dg)
    da_ref[...] = nn(hi, suffix) + nn(mid, suffix) + nn(lo, suffix)


def pack_kernel(hop_ref, ret_ref, da_ref, out_any, scr, out_ref, sems, *, used):
    total = hop_ref[0].astype(F32)
    for p in range(1, 4):
        total += hop_ref[p].astype(F32)
    rows = total.shape[0] + da_ref.shape[0]
    small = [total, da_ref[...], jnp.zeros((L - rows, L), F32)]
    scr[...] = ret_ref[...]
    scr[:, used, :] = jnp.concatenate(small, axis=0).T
    scr[:, used + 1, :] = jnp.zeros((L, L), F32)
    send_out(scr, out_ref, out_any, sems)


def final_kernel(back_ref, dx_ref, tis_ref, mine_ref, other_ref, gx_ref, iu_ref, iv_ref, cu_ref, cv_ref, da_ref, scr, *, heads):
    n = dx_ref.shape[1]
    blocks = n // L
    halves = heads // 2
    keep = keep_of(tis_ref[...], n)
    scr[...] = back_ref[...].astype(F32)
    for k in range(blocks):
        at = pl.ds(k * L, L)
        for r in range(halves):
            ch = pl.ds(r * L, L)
            both = dx_ref[ch, at] + scr[:, halves * k + r, :].T
            gx_ref[ch, at] = (both * keep[:, k * L : (k + 1) * L]).astype(BF16)
    small = scr[:, halves * blocks, :].T
    quarter = cu_ref.shape[0]
    for k in range(blocks):
        at = pl.ds(k * L, L)
        o = 2 * quarter * k
        cu_ref[:, at] = small[o : o + quarter].astype(BF16)
        cv_ref[:, at] = small[o + quarter : o + 2 * quarter].astype(BF16)
        o = 2 * quarter * blocks + heads * k
        da_ref[:, at] = small[o : o + heads].astype(BF16)
    row = mine_ref[...] + other_ref[...].astype(F32)
    iu_ref[...] = row[:quarter].astype(BF16)
    iv_ref[...] = row[quarter:].astype(BF16)


def call(kernel, outs, scratch, flops, name, limit=32, ins=None):
    place = lambda far: pl.BlockSpec(memory_space=pl.ANY if far else pltpu.VMEM)
    more = {} if ins is None else {"in_specs": [place(far) for far in ins]}
    return pl.pallas_call(
        kernel,
        **more,
        out_shape=[jax.ShapeDtypeStruct(o[0], o[1]) for o in outs],
        out_specs=[place(len(o) > 2) for o in outs],
        scratch_shapes=scratch,
        compiler_params=pltpu.CompilerParams(vmem_limit_bytes=limit * 2**20),
        cost_estimate=pl.CostEstimate(flops=flops, bytes_accessed=10**6, transcendentals=0),
        name=name,
    )


def body(features, cotangent, inject_row, readout_row, inject_col, readout_col, decay_row, decay_col, tissue):
    heads = decay_row.shape[0]
    chan, _, n = features.shape
    nstate = inject_row.shape[0]
    quarter = nstate // 4
    blocks = n // L
    flat = lambda x: x.reshape(x.shape[0], n)
    vm, dma = pltpu.VMEM, pltpu.SemaphoreType.DMA
    x, w = flat(features), flat(cotangent)
    per = 2 * chan // L + 1
    rows_out = per * blocks + 1
    tile = (L, rows_out, L)
    (send,) = call(
        prep_kernel,
        [(tile, BF16, "far")],
        [
            vm((chan, n), BF16), vm((chan, n), BF16), vm((nstate, n), BF16), vm((nstate, n), BF16),
            vm((heads, n), BF16), vm(tissue.shape, jnp.int32), vm(tile, BF16), vm(tile, F32),
            dma((4 + 2 * chan // L,)), dma((4,)),
        ],
        10**7, "pack_rows", 60, [True] * 6,
    )(x, w, flat(inject_col), flat(readout_col), flat(decay_col), tissue)
    recv = lax.all_to_all(send, "rows", split_axis=0, concat_axis=0, tiled=True)
    share = (2 * quarter, n)
    two = (4 * quarter, n)
    dx_row, own, give, da_row = call(
        row_kernel,
        [((chan, n), F32), (two, F32), (two, BF16), ((heads, n), BF16)],
        [vm((chan, n), F32), vm((2 * nstate, n), F32), vm((chan, n), BF16), vm((chan, n), BF16), vm((n, chan), BF16)],
        4 * 10**9, "row_scan",
    )(x, w, tissue, flat(inject_row), flat(readout_row), flat(decay_row))
    near = lax.ppermute(give, "heads", [(i, i ^ 1) for i in range(4)])
    used = blocks * heads // 2
    back_tile = (L, used + 2, L)
    hop, ret, da_col, mine, give = call(
        partial(col_kernel, blocks=blocks, heads=heads),
        [((4, 2 * quarter * blocks, L), BF16), (back_tile, F32), ((16, L), F32), (share, F32), (share, BF16)],
        [vm(tile, F32), vm((L, chan), F32), vm((L, chan), F32)],
        10**9, "col_scan",
    )(recv, own, near)
    hopped = lax.all_to_all(hop, "heads", split_axis=0, concat_axis=0, tiled=True)
    other = lax.ppermute(give, "heads", [(i, i ^ 2) for i in range(4)])
    (packed,) = call(
        partial(pack_kernel, used=used),
        [(back_tile, BF16, "far")],
        [vm(back_tile, F32), vm(back_tile, BF16), dma((4,))],
        10**7, "pack_cols",
    )(hopped, ret, da_col)
    back = lax.all_to_all(packed, "rows", split_axis=0, concat_axis=0, tiled=True)
    gx, iu, iv, cu, cv, da = call(
        partial(final_kernel, heads=heads),
        [((chan, n), BF16)] + [((quarter, n), BF16)] * 4 + [((heads, n), BF16)],
        [vm(back_tile, F32)],
        10**7, "join",
    )(back, dx_row, tissue, mine, other)
    wide = lambda x: x.reshape(x.shape[0], 1, n)
    return wide(gx), wide(iu), wide(iv), wide(cu), wide(cv), wide(da_row), wide(da)


def solution(mesh):
    split = P("heads", "rows", None)
    shared = P(None, "rows", None)
    in_specs = (split, split, shared, shared, shared, shared, split, split, P("rows", None))
    return jax.shard_map(body, mesh=mesh, in_specs=in_specs, out_specs=(split,) * 7, check_vma=False)
```

```python
from functools import partial

import jax
import jax.numpy as jnp
from jax import lax
from jax.experimental import pallas as pl
from jax.experimental.pallas import tpu as pltpu
from jax.sharding import PartitionSpec as P

TILE = 16
L = 128
HD = 64
F32, BF16 = jnp.float32, jnp.bfloat16


def nn(a, b):
    return lax.dot_general(a, b, (((1,), (0,)), ((), ())), preferred_element_type=F32)


def nt(a, b):
    return lax.dot_general(a, b, (((1,), (1,)), ((), ())), preferred_element_type=F32)


def tn(a, b):
    return lax.dot_general(a, b, (((0,), (0,)), ((), ())), preferred_element_type=F32)


def upper(dtype):
    i = lax.broadcasted_iota(jnp.int32, (L, L), 0)
    j = lax.broadcasted_iota(jnp.int32, (L, L), 1)
    return (i <= j).astype(dtype)


def shuffle(rows, times):
    m = rows * times
    i = lax.broadcasted_iota(jnp.int32, (m, m), 0)
    c = lax.broadcasted_iota(jnp.int32, (m, m), 1)
    return ((c // times == i % rows) & (c % times == i // rows)).astype(BF16)


def head_lanes():
    lane = lax.broadcasted_iota(jnp.int32, (1, L), 1)
    return (lane < HD).astype(BF16), (lane >= HD).astype(BF16)


def split3(x):
    hi = x.astype(BF16)
    r = x - hi.astype(F32)
    mid = r.astype(BF16)
    return hi, mid, (r - mid.astype(F32)).astype(BF16)


def keep_of(tissue, n):
    tiles = tissue.shape[1]
    t = lax.broadcasted_iota(jnp.int32, (tiles, n), 0) * TILE
    j = lax.broadcasted_iota(jnp.int32, (tiles, n), 1)
    spread = ((j >= t) & (j < t + TILE)).astype(F32)
    rows = jnp.broadcast_to(tissue.astype(F32), (8, tiles))
    return nn(rows, spread)[0:1]


def prep_kernel(x_any, w_any, u_any, v_any, a_any, tis_any, send_any, x_ref, w_ref, u_ref, v_ref, a_ref, tis_ref, send_ref, sems, out_sems):
    n = x_ref.shape[1]
    blocks = n // L
    halves = x_ref.shape[0] // L
    per = 2 * halves + 1
    heads = a_ref.shape[0]
    pairs = [(tis_any, tis_ref), (u_any, u_ref), (v_any, v_ref), (a_any, a_ref)]
    for whole, mine in ((x_any, x_ref), (w_any, w_ref)):
        pairs += [(whole.at[pl.ds(r * L, L)], mine.at[pl.ds(r * L, L)]) for r in range(halves)]
    copies = [pltpu.make_async_copy(src, dst, sems.at[i]) for i, (src, dst) in enumerate(pairs)]
    for copy in copies:
        copy.start()
    for copy in copies[:4]:
        copy.wait()
    keep = keep_of(tis_ref[...], n).astype(BF16)
    rows_of = [None] * (per * blocks + 1)
    for k in range(blocks):
        at = pl.ds(k * L, L)
        uv = jnp.concatenate([u_ref[:, at].astype(F32), v_ref[:, at].astype(F32)], axis=0)
        rows_of[per * k + 2 * halves] = uv.T
    a = [a_ref[:, pl.ds(k * L, L)].astype(F32) for k in range(blocks)]
    a.append(jnp.zeros((L - heads * blocks, L), F32))
    rows_of[per * blocks] = jnp.concatenate(a, axis=0).T
    for o, ref in ((0, x_ref), (halves, w_ref)):
        for r in range(halves):
            copies[4 + o + r].wait()
            for k in range(blocks):
                at = pl.ds(k * L, L)
                part = ref[pl.ds(r * L, L), at] * keep[:, k * L : (k + 1) * L]
                rows_of[per * k + o + r] = part.T.astype(F32)
    send_tiles(rows_of, send_ref, send_any, out_sems)


def send_out(src, mid, dst, sems):
    pieces = sems.shape[0]
    size = src.shape[0] // pieces
    copies = []
    for i in range(pieces):
        at = pl.ds(i * size, size)
        mid[at] = src[at].astype(mid.dtype)
        copies.append(pltpu.make_async_copy(mid.at[at], dst.at[at], sems.at[i]))
        copies[-1].start()
    for copy in copies:
        copy.wait()


def send_tiles(planes, mid, dst, sems):
    rows, pieces = len(planes), sems.shape[0]
    size = L // rows
    order = shuffle(rows, size)
    copies = []
    for i in range(pieces):
        for g in range(rows // pieces):
            at = (i * (rows // pieces) + g) * size
            mixed = jnp.concatenate([p[at : at + size] for p in planes], axis=0)
            mid[pl.ds(at, size)] = nn(order, mixed.astype(BF16)).astype(BF16).reshape(size, rows, L)
        at = pl.ds(i * (L // pieces), L // pieces)
        copies.append(pltpu.make_async_copy(mid.at[at], dst.at[at], sems.at[i]))
        copies[-1].start()
    for copy in copies:
        copy.wait()


def planes_of(ref):
    rows = ref.shape[1]
    size = L // rows
    order = shuffle(size, rows)
    parts = [nn(order, ref[pl.ds(g * size, size)].reshape(L, L)) for g in range(rows)]
    return [jnp.concatenate([p[j * size : (j + 1) * size] for p in parts], axis=0) for j in range(rows)]


def row_kernel(x_ref, w_ref, tis_ref, u_ref, v_ref, a_ref, dx_ref, own_ref, give_ref, da_ref, y_ref, duv_ref, xm_ref, wm_ref, wt_ref):
    n = x_ref.shape[1]
    keep = keep_of(tis_ref[...], n).astype(BF16)
    xm_ref[...] = x_ref[...] * keep
    wm_ref[...] = w_ref[...] * keep
    for b in range(n // L):
        for r in range(x_ref.shape[0] // L):
            wt_ref[pl.ds(b * L, L), pl.ds(r * L, L)] = wm_ref[pl.ds(r * L, L), pl.ds(b * L, L)].astype(F32).T.astype(BF16)
    blocks = n // L
    heads = a_ref.shape[0]
    nstate = u_ref.shape[0]
    tri = upper(BF16)
    le = upper(F32)
    carry = jnp.zeros((heads, 1), F32)
    grow, gcol = [], []
    for b in range(blocks):
        g = nn(a_ref[:, pl.ds(b * L, L)], tri) + carry
        carry = g[:, L - 1 : L]
        grow.append(g)
        gcol.append(jnp.concatenate([g, jnp.zeros((8 - heads, L), F32)], axis=0).T)
    vt = [v_ref[:, pl.ds(b * L, L)].astype(F32).T.astype(BF16) for b in range(blocks)]
    i0 = lax.broadcasted_iota(jnp.int32, (L, L), 0)
    i1 = lax.broadcasted_iota(jnp.int32, (L, L), 1)
    lower = i1 <= i0
    dv = [None] * blocks
    du = [None] * blocks
    for j in range(blocks):
        sj = pl.ds(j * L, L)
        dxs = [None] * heads
        for i in range(j, blocks):
            ti = pl.ds(i * L, L)
            s = nn(vt[i], u_ref[:, sj])
            q = None
            for h in range(heads):
                ch = pl.ds(h * HD, HD)
                d = jnp.exp(jnp.minimum(gcol[i][:, h : h + 1] - grow[j][h : h + 1, :], 0.0))
                if i == j:
                    d = jnp.where(lower, d, 0.0)
                m = nn(wt_ref[ti, ch], xm_ref[ch, sj])
                dm = d * m
                q = dm if q is None else q + dm
                a = (d * s).astype(BF16)
                part = nn(wm_ref[ch, ti], a)
                dxs[h] = part if dxs[h] is None else dxs[h] + part
                y = nt(xm_ref[ch, sj], a)
                if j == 0:
                    y_ref[ch, ti] = y
                else:
                    y_ref[ch, ti] += y
            qb = q.astype(BF16)
            pu = nn(v_ref[:, ti], qb)
            pv = nt(u_ref[:, sj], qb)
            du[j] = pu if du[j] is None else du[j] + pu
            dv[i] = pv if dv[i] is None else dv[i] + pv
        for h in range(heads):
            dx_ref[pl.ds(h * HD, HD), sj] = dxs[h]
    quarter = nstate // 4
    for b in range(blocks):
        at = pl.ds(b * L, L)
        for k in range(4):
            duv_ref[pl.ds(2 * quarter * k, quarter), at] = du[b][quarter * k : quarter * (k + 1)]
            duv_ref[pl.ds(2 * quarter * k + quarter, quarter), at] = dv[b][quarter * k : quarter * (k + 1)]
    me = lax.axis_index("heads")
    part = 2 * quarter
    for slot, near in enumerate((me, lax.rem(me + 2, 4))):
        far = near + 1 - 2 * lax.rem(near, 2)
        to = pl.ds(slot * part, part)
        own_ref[to, :] = duv_ref[pl.ds(pl.multiple_of(near * part, part), part), :]
        give_ref[to, :] = duv_ref[pl.ds(pl.multiple_of(far * part, part), part), :].astype(give_ref.dtype)
    suffix = (i0 >= i1).astype(BF16)
    later = jnp.zeros((heads, 1), F32)
    for b in reversed(range(blocks)):
        at = pl.ds(b * L, L)
        e = wm_ref[:, at].astype(F32) * y_ref[:, at] - xm_ref[:, at].astype(F32) * dx_ref[:, at]
        dg = jnp.sum(e.reshape(heads, HD, L), axis=1)
        hi, mid, lo = split3(dg)
        da = nn(hi, suffix) + nn(mid, suffix) + nn(lo, suffix) + later
        later = da[:, 0:1]
        da_ref[:, at] = da.astype(BF16)


def col_kernel(recv_ref, own_ref, near_ref, hop_ref, ret_ref, da_ref, mine_ref, pass_ref, y_ref, dx_ref, *, blocks, heads):
    part = mine_ref.shape[0]
    mine_ref[...] = own_ref[:part] + near_ref[:part].astype(F32)
    pass_ref[...] = (own_ref[part:] + near_ref[part:].astype(F32)).astype(pass_ref.dtype)
    mat = planes_of(recv_ref)
    halves = heads // 2
    per = 2 * halves + 1
    half = head_lanes()
    i0 = lax.broadcasted_iota(jnp.int32, (L, L), 0)
    i1 = lax.broadcasted_iota(jnp.int32, (L, L), 1)
    later = i0 <= i1
    gcol = nn((i1 <= i0).astype(BF16), mat[per * blocks].astype(BF16))
    grow = gcol.T
    quarter = HD // 4
    rows = da_ref.shape[0]
    width = heads * HD
    c0 = lax.broadcasted_iota(jnp.int32, (rows, width), 0)
    c1 = lax.broadcasted_iota(jnp.int32, (rows, width), 1)
    dg = jnp.zeros((rows, L), F32)
    for k in range(blocks):
        uvt = mat[per * k + 2 * halves]
        uv = uvt.T.astype(BF16)
        u, v = uv[:HD], uv[HD:]
        s = nn(uvt[:, :HD].astype(BF16), v)
        q = None
        xs = [mat[per * k + r] for r in range(halves)]
        ws = [mat[per * k + halves + r] for r in range(halves)]
        for r in range(halves):
            pair = pl.ds(r * L, L)
            x, w = xs[r].astype(BF16), ws[r].astype(BF16)
            x_of = [x * half[0], x * half[1]]
            w_of = [w * half[0], w * half[1]]
            a = []
            for h in range(2):
                c = heads * k + 2 * r + h
                d = jnp.exp(jnp.minimum(grow[c : c + 1, :] - gcol[:, c : c + 1], 0.0))
                d = jnp.where(later, d, 0.0)
                dm = d * nt(x_of[h], w)
                q = dm if q is None else q + dm
                a.append((d * s).astype(BF16))
            dx_ref[:, pair] = nn(jnp.concatenate(a, axis=1), jnp.concatenate(w_of, axis=0))
            y_ref[:, pair] = tn(jnp.concatenate(a, axis=0), jnp.concatenate(x_of, axis=0))
        qb = q.astype(BF16)
        du = nt(v, qb).astype(BF16)
        dv = nn(u, qb).astype(BF16)
        for p in range(4):
            hop_ref[p, pl.ds(2 * quarter * k, quarter), :] = du[quarter * p : quarter * (p + 1)]
            hop_ref[p, pl.ds(2 * quarter * k + quarter, quarter), :] = dv[quarter * p : quarter * (p + 1)]
        dx = dx_ref[...]
        for r in range(halves):
            ret_ref[:, halves * k + r, :] = dx[:, r * L : (r + 1) * L]
        e = jnp.concatenate(ws, axis=1) * y_ref[...] - jnp.concatenate(xs, axis=1) * dx
        start = (c0 - heads * k) * HD
        seg = ((c1 >= start) & (c1 < start + HD)).astype(BF16)
        for term in split3(e):
            dg += nt(seg, term)
    suffix = (i0 >= i1).astype(BF16)
    hi, mid, lo = split3(dg)
    da_ref[...] = nn(hi, suffix) + nn(mid, suffix) + nn(lo, suffix)


def pack_kernel(hop_ref, ret_ref, da_ref, out_any, scr, out_ref, sems, *, used):
    total = hop_ref[0].astype(F32)
    for p in range(1, 4):
        total += hop_ref[p].astype(F32)
    rows = total.shape[0] + da_ref.shape[0]
    small = [total, da_ref[...], jnp.zeros((L - rows, L), F32)]
    scr[...] = ret_ref[...]
    scr[:, used, :] = jnp.concatenate(small, axis=0).T
    scr[:, used + 1, :] = jnp.zeros((L, L), F32)
    send_out(scr, out_ref, out_any, sems)


def final_kernel(back_ref, dx_ref, tis_ref, mine_ref, other_ref, gx_ref, iu_ref, iv_ref, cu_ref, cv_ref, da_ref, scr, *, heads):
    n = dx_ref.shape[1]
    blocks = n // L
    halves = heads // 2
    keep = keep_of(tis_ref[...], n)
    scr[...] = back_ref[...].astype(F32)
    for k in range(blocks):
        at = pl.ds(k * L, L)
        for r in range(halves):
            ch = pl.ds(r * L, L)
            both = dx_ref[ch, at] + scr[:, halves * k + r, :].T
            gx_ref[ch, at] = (both * keep[:, k * L : (k + 1) * L]).astype(BF16)
    small = scr[:, halves * blocks, :].T
    quarter = cu_ref.shape[0]
    for k in range(blocks):
        at = pl.ds(k * L, L)
        o = 2 * quarter * k
        cu_ref[:, at] = small[o : o + quarter].astype(BF16)
        cv_ref[:, at] = small[o + quarter : o + 2 * quarter].astype(BF16)
        o = 2 * quarter * blocks + heads * k
        da_ref[:, at] = small[o : o + heads].astype(BF16)
    row = mine_ref[...] + other_ref[...].astype(F32)
    iu_ref[...] = row[:quarter].astype(BF16)
    iv_ref[...] = row[quarter:].astype(BF16)


def call(kernel, outs, scratch, flops, name, limit=32, ins=None):
    place = lambda far: pl.BlockSpec(memory_space=pl.ANY if far else pltpu.VMEM)
    more = {} if ins is None else {"in_specs": [place(far) for far in ins]}
    return pl.pallas_call(
        kernel,
        **more,
        out_shape=[jax.ShapeDtypeStruct(o[0], o[1]) for o in outs],
        out_specs=[place(len(o) > 2) for o in outs],
        scratch_shapes=scratch,
        compiler_params=pltpu.CompilerParams(vmem_limit_bytes=limit * 2**20),
        cost_estimate=pl.CostEstimate(flops=flops, bytes_accessed=10**6, transcendentals=0),
        name=name,
    )


def body(features, cotangent, inject_row, readout_row, inject_col, readout_col, decay_row, decay_col, tissue):
    heads = decay_row.shape[0]
    chan, _, n = features.shape
    nstate = inject_row.shape[0]
    quarter = nstate // 4
    blocks = n // L
    flat = lambda x: x.reshape(x.shape[0], n)
    vm, dma = pltpu.VMEM, pltpu.SemaphoreType.DMA
    x, w = flat(features), flat(cotangent)
    per = 2 * chan // L + 1
    rows_out = per * blocks + 1
    tile = (L, rows_out, L)
    (send,) = call(
        prep_kernel,
        [(tile, BF16, "far")],
        [
            vm((chan, n), BF16), vm((chan, n), BF16), vm((nstate, n), BF16), vm((nstate, n), BF16),
            vm((heads, n), BF16), vm(tissue.shape, jnp.int32), vm(tile, BF16),
            dma((4 + 2 * chan // L,)), dma((4,)),
        ],
        10**7, "pack_rows", 60, [True] * 6,
    )(x, w, flat(inject_col), flat(readout_col), flat(decay_col), tissue)
    recv = lax.all_to_all(send, "rows", split_axis=0, concat_axis=0, tiled=True)
    share = (2 * quarter, n)
    two = (4 * quarter, n)
    dx_row, own, give, da_row = call(
        row_kernel,
        [((chan, n), F32), (two, F32), (two, BF16), ((heads, n), BF16)],
        [vm((chan, n), F32), vm((2 * nstate, n), F32), vm((chan, n), BF16), vm((chan, n), BF16), vm((n, chan), BF16)],
        4 * 10**9, "row_scan",
    )(x, w, tissue, flat(inject_row), flat(readout_row), flat(decay_row))
    near = lax.ppermute(give, "heads", [(i, i ^ 1) for i in range(4)])
    used = blocks * heads // 2
    back_tile = (L, used + 2, L)
    hop, ret, da_col, mine, give = call(
        partial(col_kernel, blocks=blocks, heads=heads),
        [((4, 2 * quarter * blocks, L), BF16), (back_tile, F32), ((16, L), F32), (share, F32), (share, BF16)],
        [vm((L, chan), F32), vm((L, chan), F32)],
        10**9, "col_scan",
    )(recv, own, near)
    hopped = lax.all_to_all(hop, "heads", split_axis=0, concat_axis=0, tiled=True)
    other = lax.ppermute(give, "heads", [(i, i ^ 2) for i in range(4)])
    (packed,) = call(
        partial(pack_kernel, used=used),
        [(back_tile, BF16, "far")],
        [vm(back_tile, F32), vm(back_tile, BF16), dma((4,))],
        10**7, "pack_cols",
    )(hopped, ret, da_col)
    back = lax.all_to_all(packed, "rows", split_axis=0, concat_axis=0, tiled=True)
    gx, iu, iv, cu, cv, da = call(
        partial(final_kernel, heads=heads),
        [((chan, n), BF16)] + [((quarter, n), BF16)] * 4 + [((heads, n), BF16)],
        [vm(back_tile, F32)],
        10**7, "join",
    )(back, dx_row, tissue, mine, other)
    wide = lambda x: x.reshape(x.shape[0], 1, n)
    return wide(gx), wide(iu), wide(iv), wide(cu), wide(cv), wide(da_row), wide(da)


def solution(mesh):
    split = P("heads", "rows", None)
    shared = P(None, "rows", None)
    in_specs = (split, split, shared, shared, shared, shared, split, split, P("rows", None))
    return jax.shard_map(body, mesh=mesh, in_specs=in_specs, out_specs=(split,) * 7, check_vma=False)
```

```python
from functools import partial

import jax
import jax.numpy as jnp
from jax import lax
from jax.experimental import pallas as pl
from jax.experimental.pallas import tpu as pltpu
from jax.sharding import PartitionSpec as P

TILE = 16
L = 128
HD = 64
F32, BF16 = jnp.float32, jnp.bfloat16


def nn(a, b):
    return lax.dot_general(a, b, (((1,), (0,)), ((), ())), preferred_element_type=F32)


def nt(a, b):
    return lax.dot_general(a, b, (((1,), (1,)), ((), ())), preferred_element_type=F32)


def tn(a, b):
    return lax.dot_general(a, b, (((0,), (0,)), ((), ())), preferred_element_type=F32)


def upper(dtype):
    i = lax.broadcasted_iota(jnp.int32, (L, L), 0)
    j = lax.broadcasted_iota(jnp.int32, (L, L), 1)
    return (i <= j).astype(dtype)


def shuffle(rows, times):
    m = rows * times
    i = lax.broadcasted_iota(jnp.int32, (m, m), 0)
    c = lax.broadcasted_iota(jnp.int32, (m, m), 1)
    return ((c // times == i % rows) & (c % times == i // rows)).astype(BF16)


def head_lanes():
    lane = lax.broadcasted_iota(jnp.int32, (1, L), 1)
    return (lane < HD).astype(BF16), (lane >= HD).astype(BF16)


def split3(x):
    hi = x.astype(BF16)
    r = x - hi.astype(F32)
    mid = r.astype(BF16)
    return hi, mid, (r - mid.astype(F32)).astype(BF16)


def keep_of(tissue, n):
    tiles = tissue.shape[1]
    t = lax.broadcasted_iota(jnp.int32, (tiles, n), 0) * TILE
    j = lax.broadcasted_iota(jnp.int32, (tiles, n), 1)
    spread = ((j >= t) & (j < t + TILE)).astype(F32)
    rows = jnp.broadcast_to(tissue.astype(F32), (8, tiles))
    return nn(rows, spread)[0:1]


def prep_kernel(x_any, w_any, u_any, v_any, a_any, tis_any, send_any, x_ref, w_ref, u_ref, v_ref, a_ref, tis_ref, send_ref, sems, out_sems):
    n = x_ref.shape[1]
    blocks = n // L
    halves = x_ref.shape[0] // L
    per = 2 * halves + 1
    heads = a_ref.shape[0]
    pairs = [(tis_any, tis_ref), (u_any, u_ref), (v_any, v_ref), (a_any, a_ref)]
    for whole, mine in ((x_any, x_ref), (w_any, w_ref)):
        pairs += [(whole.at[pl.ds(r * L, L)], mine.at[pl.ds(r * L, L)]) for r in range(halves)]
    copies = [pltpu.make_async_copy(src, dst, sems.at[i]) for i, (src, dst) in enumerate(pairs)]
    for copy in copies:
        copy.start()
    for copy in copies[:4]:
        copy.wait()
    keep = keep_of(tis_ref[...], n).astype(BF16)
    rows_of = [None] * (per * blocks + 1)
    for k in range(blocks):
        at = pl.ds(k * L, L)
        uv = jnp.concatenate([u_ref[:, at].astype(F32), v_ref[:, at].astype(F32)], axis=0)
        rows_of[per * k + 2 * halves] = uv.T
    a = [a_ref[:, pl.ds(k * L, L)].astype(F32) for k in range(blocks)]
    a.append(jnp.zeros((L - heads * blocks, L), F32))
    rows_of[per * blocks] = jnp.concatenate(a, axis=0).T
    for o, ref in ((0, x_ref), (halves, w_ref)):
        for r in range(halves):
            copies[4 + o + r].wait()
            for k in range(blocks):
                at = pl.ds(k * L, L)
                part = ref[pl.ds(r * L, L), at] * keep[:, k * L : (k + 1) * L]
                rows_of[per * k + o + r] = part.T.astype(F32)
    send_tiles(rows_of, send_ref, send_any, out_sems)


def send_out(src, mid, dst, sems):
    pieces = sems.shape[0]
    size = src.shape[0] // pieces
    copies = []
    for i in range(pieces):
        at = pl.ds(i * size, size)
        mid[at] = src[at].astype(mid.dtype)
        copies.append(pltpu.make_async_copy(mid.at[at], dst.at[at], sems.at[i]))
        copies[-1].start()
    for copy in copies:
        copy.wait()


def send_tiles(planes, mid, dst, sems):
    rows, pieces = len(planes), sems.shape[0]
    size = L // rows
    order = shuffle(rows, size)
    copies = []
    for i in range(pieces):
        for g in range(rows // pieces):
            at = (i * (rows // pieces) + g) * size
            mixed = jnp.concatenate([p[at : at + size] for p in planes], axis=0)
            mid[pl.ds(at, size)] = nn(order, mixed.astype(BF16)).astype(BF16).reshape(size, rows, L)
        at = pl.ds(i * (L // pieces), L // pieces)
        copies.append(pltpu.make_async_copy(mid.at[at], dst.at[at], sems.at[i]))
        copies[-1].start()
    for copy in copies:
        copy.wait()


def planes_of(ref):
    rows = ref.shape[1]
    size = L // rows
    order = shuffle(size, rows)
    parts = [nn(order, ref[pl.ds(g * size, size)].reshape(L, L)) for g in range(rows)]
    return [jnp.concatenate([p[j * size : (j + 1) * size] for p in parts], axis=0) for j in range(rows)]


def row_kernel(x_ref, w_ref, tis_ref, u_ref, v_ref, a_ref, dx_ref, d0_ref, d1_ref, d2_ref, d3_ref, da_ref, y_ref, duv_ref, xm_ref, wm_ref, wt_ref):
    n = x_ref.shape[1]
    keep = keep_of(tis_ref[...], n).astype(BF16)
    xm_ref[...] = x_ref[...] * keep
    wm_ref[...] = w_ref[...] * keep
    for b in range(n // L):
        for r in range(x_ref.shape[0] // L):
            wt_ref[pl.ds(b * L, L), pl.ds(r * L, L)] = wm_ref[pl.ds(r * L, L), pl.ds(b * L, L)].astype(F32).T.astype(BF16)
    blocks = n // L
    heads = a_ref.shape[0]
    nstate = u_ref.shape[0]
    tri = upper(BF16)
    le = upper(F32)
    carry = jnp.zeros((heads, 1), F32)
    grow, gcol = [], []
    for b in range(blocks):
        g = nn(a_ref[:, pl.ds(b * L, L)], tri) + carry
        carry = g[:, L - 1 : L]
        grow.append(g)
        gcol.append(jnp.concatenate([g, jnp.zeros((8 - heads, L), F32)], axis=0).T)
    vt = [v_ref[:, pl.ds(b * L, L)].astype(F32).T.astype(BF16) for b in range(blocks)]
    i0 = lax.broadcasted_iota(jnp.int32, (L, L), 0)
    i1 = lax.broadcasted_iota(jnp.int32, (L, L), 1)
    lower = i1 <= i0
    dv = [None] * blocks
    du = [None] * blocks
    for j in range(blocks):
        sj = pl.ds(j * L, L)
        dxs = [None] * heads
        for i in range(j, blocks):
            ti = pl.ds(i * L, L)
            s = nn(vt[i], u_ref[:, sj])
            q = None
            for h in range(heads):
                ch = pl.ds(h * HD, HD)
                d = jnp.exp(jnp.minimum(gcol[i][:, h : h + 1] - grow[j][h : h + 1, :], 0.0))
                if i == j:
                    d = jnp.where(lower, d, 0.0)
                m = nn(wt_ref[ti, ch], xm_ref[ch, sj])
                dm = d * m
                q = dm if q is None else q + dm
                a = (d * s).astype(BF16)
                part = nn(wm_ref[ch, ti], a)
                dxs[h] = part if dxs[h] is None else dxs[h] + part
                y = nt(xm_ref[ch, sj], a)
                if j == 0:
                    y_ref[ch, ti] = y
                else:
                    y_ref[ch, ti] += y
            qb = q.astype(BF16)
            pu = nn(v_ref[:, ti], qb)
            pv = nt(u_ref[:, sj], qb)
            du[j] = pu if du[j] is None else du[j] + pu
            dv[i] = pv if dv[i] is None else dv[i] + pv
        for h in range(heads):
            dx_ref[pl.ds(h * HD, HD), sj] = dxs[h]
    quarter = nstate // 4
    for b in range(blocks):
        at = pl.ds(b * L, L)
        for k in range(4):
            duv_ref[pl.ds(2 * quarter * k, quarter), at] = du[b][quarter * k : quarter * (k + 1)]
            duv_ref[pl.ds(2 * quarter * k + quarter, quarter), at] = dv[b][quarter * k : quarter * (k + 1)]
    me = lax.axis_index("heads")
    for shift, ref in enumerate((d0_ref, d1_ref, d2_ref, d3_ref)):
        part = lax.rem(me + shift, 4) * (2 * quarter)
        ref[...] = duv_ref[pl.ds(pl.multiple_of(part, 2 * quarter), 2 * quarter), :].astype(ref.dtype)
    suffix = (i0 >= i1).astype(BF16)
    later = jnp.zeros((heads, 1), F32)
    for b in reversed(range(blocks)):
        at = pl.ds(b * L, L)
        e = wm_ref[:, at].astype(F32) * y_ref[:, at] - xm_ref[:, at].astype(F32) * dx_ref[:, at]
        dg = jnp.sum(e.reshape(heads, HD, L), axis=1)
        hi, mid, lo = split3(dg)
        da = nn(hi, suffix) + nn(mid, suffix) + nn(lo, suffix) + later
        later = da[:, 0:1]
        da_ref[:, at] = da.astype(BF16)


def col_kernel(recv_ref, after_ref, hop_ref, ret_ref, da_ref, y_ref, dx_ref, *, blocks, heads):
    mat = planes_of(recv_ref)
    halves = heads // 2
    per = 2 * halves + 1
    half = head_lanes()
    i0 = lax.broadcasted_iota(jnp.int32, (L, L), 0)
    i1 = lax.broadcasted_iota(jnp.int32, (L, L), 1)
    later = i0 <= i1
    gcol = nn((i1 <= i0).astype(BF16), mat[per * blocks].astype(BF16))
    grow = gcol.T
    quarter = HD // 4
    rows = da_ref.shape[0]
    width = heads * HD
    c0 = lax.broadcasted_iota(jnp.int32, (rows, width), 0)
    c1 = lax.broadcasted_iota(jnp.int32, (rows, width), 1)
    dg = jnp.zeros((rows, L), F32)
    for k in range(blocks):
        uvt = mat[per * k + 2 * halves]
        uv = uvt.T.astype(BF16)
        u, v = uv[:HD], uv[HD:]
        s = nn(uvt[:, :HD].astype(BF16), v)
        q = None
        xs = [mat[per * k + r] for r in range(halves)]
        ws = [mat[per * k + halves + r] for r in range(halves)]
        for r in range(halves):
            pair = pl.ds(r * L, L)
            x, w = xs[r].astype(BF16), ws[r].astype(BF16)
            x_of = [x * half[0], x * half[1]]
            w_of = [w * half[0], w * half[1]]
            a = []
            for h in range(2):
                c = heads * k + 2 * r + h
                d = jnp.exp(jnp.minimum(grow[c : c + 1, :] - gcol[:, c : c + 1], 0.0))
                d = jnp.where(later, d, 0.0)
                dm = d * nt(x_of[h], w)
                q = dm if q is None else q + dm
                a.append((d * s).astype(BF16))
            dx_ref[:, pair] = nn(jnp.concatenate(a, axis=1), jnp.concatenate(w_of, axis=0))
            y_ref[:, pair] = tn(jnp.concatenate(a, axis=0), jnp.concatenate(x_of, axis=0))
        qb = q.astype(BF16)
        du = nt(v, qb).astype(BF16)
        dv = nn(u, qb).astype(BF16)
        for p in range(4):
            hop_ref[p, pl.ds(2 * quarter * k, quarter), :] = du[quarter * p : quarter * (p + 1)]
            hop_ref[p, pl.ds(2 * quarter * k + quarter, quarter), :] = dv[quarter * p : quarter * (p + 1)]
        dx = dx_ref[...]
        for r in range(halves):
            ret_ref[:, halves * k + r, :] = dx[:, r * L : (r + 1) * L]
        e = jnp.concatenate(ws, axis=1) * y_ref[...] - jnp.concatenate(xs, axis=1) * dx
        start = (c0 - heads * k) * HD
        seg = ((c1 >= start) & (c1 < start + HD)).astype(BF16)
        for term in split3(e):
            dg += nt(seg, term)
    suffix = (i0 >= i1).astype(BF16)
    hi, mid, lo = split3(dg)
    da_ref[...] = nn(hi, suffix) + nn(mid, suffix) + nn(lo, suffix)


def pack_kernel(hop_ref, ret_ref, da_ref, out_any, scr, out_ref, sems, *, used):
    total = hop_ref[0].astype(F32)
    for p in range(1, 4):
        total += hop_ref[p].astype(F32)
    rows = total.shape[0] + da_ref.shape[0]
    small = [total, da_ref[...], jnp.zeros((L - rows, L), F32)]
    scr[...] = ret_ref[...]
    scr[:, used, :] = jnp.concatenate(small, axis=0).T
    scr[:, used + 1, :] = jnp.zeros((L, L), F32)
    send_out(scr, out_ref, out_any, sems)


def final_kernel(back_ref, dx_ref, tis_ref, r0_ref, r1_ref, r2_ref, r3_ref, gx_ref, iu_ref, iv_ref, cu_ref, cv_ref, da_ref, scr, *, heads):
    n = dx_ref.shape[1]
    blocks = n // L
    halves = heads // 2
    keep = keep_of(tis_ref[...], n)
    scr[...] = back_ref[...].astype(F32)
    for k in range(blocks):
        at = pl.ds(k * L, L)
        for r in range(halves):
            ch = pl.ds(r * L, L)
            both = dx_ref[ch, at] + scr[:, halves * k + r, :].T
            gx_ref[ch, at] = (both * keep[:, k * L : (k + 1) * L]).astype(BF16)
    small = scr[:, halves * blocks, :].T
    quarter = cu_ref.shape[0]
    for k in range(blocks):
        at = pl.ds(k * L, L)
        o = 2 * quarter * k
        cu_ref[:, at] = small[o : o + quarter].astype(BF16)
        cv_ref[:, at] = small[o + quarter : o + 2 * quarter].astype(BF16)
        o = 2 * quarter * blocks + heads * k
        da_ref[:, at] = small[o : o + heads].astype(BF16)
    row = r0_ref[...] + r1_ref[...].astype(F32) + r2_ref[...].astype(F32) + r3_ref[...].astype(F32)
    iu_ref[...] = row[:quarter].astype(BF16)
    iv_ref[...] = row[quarter:].astype(BF16)


def call(kernel, outs, scratch, flops, name, limit=32, ins=None):
    place = lambda far: pl.BlockSpec(memory_space=pl.ANY if far else pltpu.VMEM)
    more = {} if ins is None else {"in_specs": [place(far) for far in ins]}
    return pl.pallas_call(
        kernel,
        **more,
        out_shape=[jax.ShapeDtypeStruct(o[0], o[1]) for o in outs],
        out_specs=[place(len(o) > 2) for o in outs],
        scratch_shapes=scratch,
        compiler_params=pltpu.CompilerParams(vmem_limit_bytes=limit * 2**20),
        cost_estimate=pl.CostEstimate(flops=flops, bytes_accessed=10**6, transcendentals=0),
        name=name,
    )


def body(features, cotangent, inject_row, readout_row, inject_col, readout_col, decay_row, decay_col, tissue):
    heads = decay_row.shape[0]
    chan, _, n = features.shape
    nstate = inject_row.shape[0]
    quarter = nstate // 4
    blocks = n // L
    flat = lambda x: x.reshape(x.shape[0], n)
    vm, dma = pltpu.VMEM, pltpu.SemaphoreType.DMA
    x, w = flat(features), flat(cotangent)
    per = 2 * chan // L + 1
    rows_out = per * blocks + 1
    tile = (L, rows_out, L)
    (send,) = call(
        prep_kernel,
        [(tile, BF16, "far")],
        [
            vm((chan, n), BF16), vm((chan, n), BF16), vm((nstate, n), BF16), vm((nstate, n), BF16),
            vm((heads, n), BF16), vm(tissue.shape, jnp.int32), vm(tile, BF16),
            dma((4 + 2 * chan // L,)), dma((4,)),
        ],
        10**7, "pack_rows", 60, [True] * 6,
    )(x, w, flat(inject_col), flat(readout_col), flat(decay_col), tissue)
    recv = lax.all_to_all(send, "rows", split_axis=0, concat_axis=0, tiled=True)
    share = (2 * quarter, n)
    dx_row, mine, *theirs, da_row = call(
        row_kernel,
        [((chan, n), F32), (share, F32), (share, BF16), (share, BF16), (share, BF16), ((heads, n), BF16)],
        [vm((chan, n), F32), vm((2 * nstate, n), F32), vm((chan, n), BF16), vm((chan, n), BF16), vm((n, chan), BF16)],
        4 * 10**9, "row_scan",
    )(x, w, tissue, flat(inject_row), flat(readout_row), flat(decay_row))
    shares = [
        lax.ppermute(part, "heads", [(i, (i + shift) % 4) for i in range(4)]) for shift, part in enumerate(theirs, 1)
    ]
    used = blocks * heads // 2
    back_tile = (L, used + 2, L)
    hop, ret, da_col = call(
        partial(col_kernel, blocks=blocks, heads=heads),
        [((4, 2 * quarter * blocks, L), BF16), (back_tile, F32), ((16, L), F32)],
        [vm((L, chan), F32), vm((L, chan), F32)],
        10**9, "col_scan",
    )(recv, da_row)
    hopped = lax.all_to_all(hop, "heads", split_axis=0, concat_axis=0, tiled=True)
    (packed,) = call(
        partial(pack_kernel, used=used),
        [(back_tile, BF16, "far")],
        [vm(back_tile, F32), vm(back_tile, BF16), dma((4,))],
        10**7, "pack_cols",
    )(hopped, ret, da_col)
    back = lax.all_to_all(packed, "rows", split_axis=0, concat_axis=0, tiled=True)
    gx, iu, iv, cu, cv, da = call(
        partial(final_kernel, heads=heads),
        [((chan, n), BF16)] + [((quarter, n), BF16)] * 4 + [((heads, n), BF16)],
        [vm(back_tile, F32)],
        10**7, "join",
    )(back, dx_row, tissue, mine, *shares)
    wide = lambda x: x.reshape(x.shape[0], 1, n)
    return wide(gx), wide(iu), wide(iv), wide(cu), wide(cv), wide(da_row), wide(da)


def solution(mesh):
    split = P("heads", "rows", None)
    shared = P(None, "rows", None)
    in_specs = (split, split, shared, shared, shared, shared, split, split, P("rows", None))
    return jax.shard_map(body, mesh=mesh, in_specs=in_specs, out_specs=(split,) * 7, check_vma=False)
```

```python
from functools import partial

import jax
import jax.numpy as jnp
from jax import lax
from jax.experimental import pallas as pl
from jax.experimental.pallas import tpu as pltpu
from jax.sharding import PartitionSpec as P

TILE = 16
L = 128
HD = 64
F32, BF16 = jnp.float32, jnp.bfloat16


def nn(a, b):
    return lax.dot_general(a, b, (((1,), (0,)), ((), ())), preferred_element_type=F32)


def nt(a, b):
    return lax.dot_general(a, b, (((1,), (1,)), ((), ())), preferred_element_type=F32)


def tn(a, b):
    return lax.dot_general(a, b, (((0,), (0,)), ((), ())), preferred_element_type=F32)


def upper(dtype):
    i = lax.broadcasted_iota(jnp.int32, (L, L), 0)
    j = lax.broadcasted_iota(jnp.int32, (L, L), 1)
    return (i <= j).astype(dtype)


def shuffle(rows, times):
    m = rows * times
    i = lax.broadcasted_iota(jnp.int32, (m, m), 0)
    c = lax.broadcasted_iota(jnp.int32, (m, m), 1)
    return ((c // times == i % rows) & (c % times == i // rows)).astype(BF16)


def head_lanes():
    lane = lax.broadcasted_iota(jnp.int32, (1, L), 1)
    return (lane < HD).astype(BF16), (lane >= HD).astype(BF16)


def split3(x):
    hi = x.astype(BF16)
    r = x - hi.astype(F32)
    mid = r.astype(BF16)
    return hi, mid, (r - mid.astype(F32)).astype(BF16)


def keep_of(tissue, n):
    tiles = tissue.shape[1]
    t = lax.broadcasted_iota(jnp.int32, (tiles, n), 0) * TILE
    j = lax.broadcasted_iota(jnp.int32, (tiles, n), 1)
    spread = ((j >= t) & (j < t + TILE)).astype(F32)
    rows = jnp.broadcast_to(tissue.astype(F32), (8, tiles))
    return nn(rows, spread)[0:1]


def prep_kernel(x_any, w_any, u_any, v_any, a_any, tis_any, send_any, x_ref, w_ref, u_ref, v_ref, a_ref, tis_ref, send_ref, sems, out_sems):
    n = x_ref.shape[1]
    blocks = n // L
    halves = x_ref.shape[0] // L
    per = 2 * halves + 1
    heads = a_ref.shape[0]
    pairs = [(tis_any, tis_ref), (u_any, u_ref), (v_any, v_ref), (a_any, a_ref)]
    for whole, mine in ((x_any, x_ref), (w_any, w_ref)):
        pairs += [(whole.at[pl.ds(r * L, L)], mine.at[pl.ds(r * L, L)]) for r in range(halves)]
    copies = [pltpu.make_async_copy(src, dst, sems.at[i]) for i, (src, dst) in enumerate(pairs)]
    for copy in copies:
        copy.start()
    for copy in copies[:4]:
        copy.wait()
    keep = keep_of(tis_ref[...], n).astype(BF16)
    rows_of = [None] * (per * blocks + 1)
    for k in range(blocks):
        at = pl.ds(k * L, L)
        uv = jnp.concatenate([u_ref[:, at].astype(F32), v_ref[:, at].astype(F32)], axis=0)
        rows_of[per * k + 2 * halves] = uv.T
    a = [a_ref[:, pl.ds(k * L, L)].astype(F32) for k in range(blocks)]
    a.append(jnp.zeros((L - heads * blocks, L), F32))
    rows_of[per * blocks] = jnp.concatenate(a, axis=0).T
    for o, ref in ((0, x_ref), (halves, w_ref)):
        for r in range(halves):
            copies[4 + o + r].wait()
            for k in range(blocks):
                at = pl.ds(k * L, L)
                part = ref[pl.ds(r * L, L), at] * keep[:, k * L : (k + 1) * L]
                rows_of[per * k + o + r] = part.T.astype(F32)
    send_tiles(rows_of, send_ref, send_any, out_sems)


def send_out(src, mid, dst, sems):
    pieces = sems.shape[0]
    size = src.shape[0] // pieces
    copies = []
    for i in range(pieces):
        at = pl.ds(i * size, size)
        mid[at] = src[at].astype(mid.dtype)
        copies.append(pltpu.make_async_copy(mid.at[at], dst.at[at], sems.at[i]))
        copies[-1].start()
    for copy in copies:
        copy.wait()


def send_tiles(planes, mid, dst, sems):
    rows, pieces = len(planes), sems.shape[0]
    size = L // rows
    order = shuffle(rows, size)
    copies = []
    for i in range(pieces):
        for g in range(rows // pieces):
            at = (i * (rows // pieces) + g) * size
            mixed = jnp.concatenate([p[at : at + size] for p in planes], axis=0)
            mid[pl.ds(at, size)] = nn(order, mixed.astype(BF16)).astype(BF16).reshape(size, rows, L)
        at = pl.ds(i * (L // pieces), L // pieces)
        copies.append(pltpu.make_async_copy(mid.at[at], dst.at[at], sems.at[i]))
        copies[-1].start()
    for copy in copies:
        copy.wait()


def planes_of(ref):
    rows = ref.shape[1]
    size = L // rows
    order = shuffle(size, rows)
    parts = [nn(order, ref[pl.ds(g * size, size)].reshape(L, L)) for g in range(rows)]
    return [jnp.concatenate([p[j * size : (j + 1) * size] for p in parts], axis=0) for j in range(rows)]


def row_kernel(x_ref, w_ref, tis_ref, u_ref, v_ref, a_ref, dx_ref, d0_ref, d1_ref, d2_ref, d3_ref, da_ref, y_ref, duv_ref, xm_ref, wm_ref, wt_ref):
    n = x_ref.shape[1]
    keep = keep_of(tis_ref[...], n).astype(BF16)
    xm_ref[...] = x_ref[...] * keep
    wm_ref[...] = w_ref[...] * keep
    for b in range(n // L):
        for r in range(x_ref.shape[0] // L):
            wt_ref[pl.ds(b * L, L), pl.ds(r * L, L)] = wm_ref[pl.ds(r * L, L), pl.ds(b * L, L)].astype(F32).T.astype(BF16)
    blocks = n // L
    heads = a_ref.shape[0]
    nstate = u_ref.shape[0]
    tri = upper(BF16)
    le = upper(F32)
    carry = jnp.zeros((heads, 1), F32)
    grow, gcol = [], []
    for b in range(blocks):
        g = nn(a_ref[:, pl.ds(b * L, L)], tri) + carry
        carry = g[:, L - 1 : L]
        grow.append(g)
        gcol.append(jnp.concatenate([g, jnp.zeros((8 - heads, L), F32)], axis=0).T)
    vt = [v_ref[:, pl.ds(b * L, L)].astype(F32).T.astype(BF16) for b in range(blocks)]
    i0 = lax.broadcasted_iota(jnp.int32, (L, L), 0)
    i1 = lax.broadcasted_iota(jnp.int32, (L, L), 1)
    lower = i1 <= i0
    dv = [None] * blocks
    du = [None] * blocks
    for j in range(blocks):
        sj = pl.ds(j * L, L)
        dxs = [None] * heads
        for i in range(j, blocks):
            ti = pl.ds(i * L, L)
            s = nn(vt[i], u_ref[:, sj])
            q = None
            for h in range(heads):
                ch = pl.ds(h * HD, HD)
                d = jnp.exp(jnp.minimum(gcol[i][:, h : h + 1] - grow[j][h : h + 1, :], 0.0))
                if i == j:
                    d = jnp.where(lower, d, 0.0)
                m = nn(wt_ref[ti, ch], xm_ref[ch, sj])
                dm = d * m
                q = dm if q is None else q + dm
                a = (d * s).astype(BF16)
                part = nn(wm_ref[ch, ti], a)
                dxs[h] = part if dxs[h] is None else dxs[h] + part
                y = nt(xm_ref[ch, sj], a)
                if j == 0:
                    y_ref[ch, ti] = y
                else:
                    y_ref[ch, ti] += y
            qb = q.astype(BF16)
            pu = nn(v_ref[:, ti], qb)
            pv = nt(u_ref[:, sj], qb)
            du[j] = pu if du[j] is None else du[j] + pu
            dv[i] = pv if dv[i] is None else dv[i] + pv
        for h in range(heads):
            dx_ref[pl.ds(h * HD, HD), sj] = dxs[h]
    quarter = nstate // 4
    for b in range(blocks):
        at = pl.ds(b * L, L)
        for k in range(4):
            duv_ref[pl.ds(2 * quarter * k, quarter), at] = du[b][quarter * k : quarter * (k + 1)]
            duv_ref[pl.ds(2 * quarter * k + quarter, quarter), at] = dv[b][quarter * k : quarter * (k + 1)]
    me = lax.axis_index("heads")
    for shift, ref in enumerate((d0_ref, d1_ref, d2_ref, d3_ref)):
        part = lax.rem(me + shift, 4) * (2 * quarter)
        ref[...] = duv_ref[pl.ds(pl.multiple_of(part, 2 * quarter), 2 * quarter), :].astype(ref.dtype)
    suffix = (i0 >= i1).astype(BF16)
    later = jnp.zeros((heads, 1), F32)
    for b in reversed(range(blocks)):
        at = pl.ds(b * L, L)
        e = wm_ref[:, at].astype(F32) * y_ref[:, at] - xm_ref[:, at].astype(F32) * dx_ref[:, at]
        dg = jnp.sum(e.reshape(heads, HD, L), axis=1)
        hi, mid, lo = split3(dg)
        da = nn(hi, suffix) + nn(mid, suffix) + nn(lo, suffix) + later
        later = da[:, 0:1]
        da_ref[:, at] = da.astype(BF16)


def col_kernel(recv_ref, after_ref, hop_ref, ret_ref, da_ref, y_ref, dx_ref, *, blocks, heads):
    mat = planes_of(recv_ref)
    halves = heads // 2
    per = 2 * halves + 1
    half = head_lanes()
    i0 = lax.broadcasted_iota(jnp.int32, (L, L), 0)
    i1 = lax.broadcasted_iota(jnp.int32, (L, L), 1)
    later = i0 <= i1
    gcol = nn((i1 <= i0).astype(BF16), mat[per * blocks].astype(BF16))
    grow = gcol.T
    quarter = HD // 4
    rows = da_ref.shape[0]
    width = heads * HD
    c0 = lax.broadcasted_iota(jnp.int32, (rows, width), 0)
    c1 = lax.broadcasted_iota(jnp.int32, (rows, width), 1)
    dg = jnp.zeros((rows, L), F32)
    for k in range(blocks):
        uvt = mat[per * k + 2 * halves]
        uv = uvt.T.astype(BF16)
        u, v = uv[:HD], uv[HD:]
        s = nn(uvt[:, :HD].astype(BF16), v)
        q = None
        xs = [mat[per * k + r] for r in range(halves)]
        ws = [mat[per * k + halves + r] for r in range(halves)]
        for r in range(halves):
            pair = pl.ds(r * L, L)
            x, w = xs[r].astype(BF16), ws[r].astype(BF16)
            x_of = [x * half[0], x * half[1]]
            w_of = [w * half[0], w * half[1]]
            a = []
            for h in range(2):
                c = heads * k + 2 * r + h
                d = jnp.exp(jnp.minimum(grow[c : c + 1, :] - gcol[:, c : c + 1], 0.0))
                d = jnp.where(later, d, 0.0)
                dm = d * nt(x_of[h], w)
                q = dm if q is None else q + dm
                a.append((d * s).astype(BF16))
            dx_ref[:, pair] = nn(jnp.concatenate(a, axis=1), jnp.concatenate(w_of, axis=0))
            y_ref[:, pair] = tn(jnp.concatenate(a, axis=0), jnp.concatenate(x_of, axis=0))
        qb = q.astype(BF16)
        du = nt(v, qb).astype(BF16)
        dv = nn(u, qb).astype(BF16)
        for p in range(4):
            hop_ref[p, pl.ds(2 * quarter * k, quarter), :] = du[quarter * p : quarter * (p + 1)]
            hop_ref[p, pl.ds(2 * quarter * k + quarter, quarter), :] = dv[quarter * p : quarter * (p + 1)]
        dx = dx_ref[...]
        for r in range(halves):
            ret_ref[:, halves * k + r, :] = dx[:, r * L : (r + 1) * L]
        e = jnp.concatenate(ws, axis=1) * y_ref[...] - jnp.concatenate(xs, axis=1) * dx
        start = (c0 - heads * k) * HD
        seg = ((c1 >= start) & (c1 < start + HD)).astype(BF16)
        for term in split3(e):
            dg += nt(seg, term)
    suffix = (i0 >= i1).astype(BF16)
    hi, mid, lo = split3(dg)
    da_ref[...] = nn(hi, suffix) + nn(mid, suffix) + nn(lo, suffix)


def pack_kernel(hop_ref, ret_ref, da_ref, out_any, scr, out_ref, sems, *, used):
    total = hop_ref[0].astype(F32)
    for p in range(1, 4):
        total += hop_ref[p].astype(F32)
    rows = total.shape[0] + da_ref.shape[0]
    small = [total, da_ref[...], jnp.zeros((L - rows, L), F32)]
    scr[...] = ret_ref[...]
    scr[:, used, :] = jnp.concatenate(small, axis=0).T
    scr[:, used + 1, :] = jnp.zeros((L, L), F32)
    send_out(scr, out_ref, out_any, sems)


def final_kernel(back_ref, dx_ref, tis_ref, r0_ref, r1_ref, r2_ref, r3_ref, gx_ref, iu_ref, iv_ref, cu_ref, cv_ref, da_ref, scr, *, heads):
    n = dx_ref.shape[1]
    blocks = n // L
    halves = heads // 2
    keep = keep_of(tis_ref[...], n)
    scr[...] = back_ref[...].astype(F32)
    for k in range(blocks):
        at = pl.ds(k * L, L)
        for r in range(halves):
            ch = pl.ds(r * L, L)
            both = dx_ref[ch, at] + scr[:, halves * k + r, :].T
            gx_ref[ch, at] = (both * keep[:, k * L : (k + 1) * L]).astype(BF16)
    small = scr[:, halves * blocks, :].T
    quarter = cu_ref.shape[0]
    for k in range(blocks):
        at = pl.ds(k * L, L)
        o = 2 * quarter * k
        cu_ref[:, at] = small[o : o + quarter].astype(BF16)
        cv_ref[:, at] = small[o + quarter : o + 2 * quarter].astype(BF16)
        o = 2 * quarter * blocks + heads * k
        da_ref[:, at] = small[o : o + heads].astype(BF16)
    row = r0_ref[...] + r1_ref[...].astype(F32) + r2_ref[...].astype(F32) + r3_ref[...].astype(F32)
    iu_ref[...] = row[:quarter].astype(BF16)
    iv_ref[...] = row[quarter:].astype(BF16)


def call(kernel, outs, scratch, flops, name, limit=32, ins=None):
    place = lambda far: pl.BlockSpec(memory_space=pl.ANY if far else pltpu.VMEM)
    more = {} if ins is None else {"in_specs": [place(far) for far in ins]}
    return pl.pallas_call(
        kernel,
        **more,
        out_shape=[jax.ShapeDtypeStruct(o[0], o[1]) for o in outs],
        out_specs=[place(len(o) > 2) for o in outs],
        scratch_shapes=scratch,
        compiler_params=pltpu.CompilerParams(vmem_limit_bytes=limit * 2**20),
        cost_estimate=pl.CostEstimate(flops=flops, bytes_accessed=10**6, transcendentals=0),
        name=name,
    )


def body(features, cotangent, inject_row, readout_row, inject_col, readout_col, decay_row, decay_col, tissue):
    heads = decay_row.shape[0]
    chan, _, n = features.shape
    nstate = inject_row.shape[0]
    quarter = nstate // 4
    blocks = n // L
    flat = lambda x: x.reshape(x.shape[0], n)
    vm, dma = pltpu.VMEM, pltpu.SemaphoreType.DMA
    x, w = flat(features), flat(cotangent)
    per = 2 * chan // L + 1
    rows_out = per * blocks + 1
    tile = (L, rows_out, L)
    (send,) = call(
        prep_kernel,
        [(tile, BF16, "far")],
        [
            vm((chan, n), BF16), vm((chan, n), BF16), vm((nstate, n), BF16), vm((nstate, n), BF16),
            vm((heads, n), BF16), vm(tissue.shape, jnp.int32), vm(tile, BF16),
            dma((4 + 2 * chan // L,)), dma((4,)),
        ],
        10**7, "pack_rows", 60, [True] * 6,
    )(x, w, flat(inject_col), flat(readout_col), flat(decay_col), tissue)
    recv = lax.all_to_all(send, "rows", split_axis=0, concat_axis=0, tiled=True)
    share = (2 * quarter, n)
    dx_row, mine, *theirs, da_row = call(
        row_kernel,
        [((chan, n), F32), (share, F32), (share, BF16), (share, BF16), (share, BF16), ((heads, n), BF16)],
        [vm((chan, n), F32), vm((2 * nstate, n), F32), vm((chan, n), BF16), vm((chan, n), BF16), vm((n, chan), BF16)],
        4 * 10**9, "row_scan",
    )(x, w, tissue, flat(inject_row), flat(readout_row), flat(decay_row))
    shares = [
        lax.ppermute(part, "heads", [(i, (i + shift) % 4) for i in range(4)]) for shift, part in enumerate(theirs, 1)
    ]
    used = blocks * heads // 2
    back_tile = (L, used + 2, L)
    hop, ret, da_col = call(
        partial(col_kernel, blocks=blocks, heads=heads),
        [((4, 2 * quarter * blocks, L), BF16), (back_tile, F32), ((16, L), F32)],
        [vm((L, chan), F32), vm((L, chan), F32)],
        10**9, "col_scan",
    )(recv, mine)
    hopped = lax.all_to_all(hop, "heads", split_axis=0, concat_axis=0, tiled=True)
    (packed,) = call(
        partial(pack_kernel, used=used),
        [(back_tile, BF16, "far")],
        [vm(back_tile, F32), vm(back_tile, BF16), dma((4,))],
        10**7, "pack_cols",
    )(hopped, ret, da_col)
    back = lax.all_to_all(packed, "rows", split_axis=0, concat_axis=0, tiled=True)
    gx, iu, iv, cu, cv, da = call(
        partial(final_kernel, heads=heads),
        [((chan, n), BF16)] + [((quarter, n), BF16)] * 4 + [((heads, n), BF16)],
        [vm(back_tile, F32)],
        10**7, "join",
    )(back, dx_row, tissue, mine, *shares)
    wide = lambda x: x.reshape(x.shape[0], 1, n)
    return wide(gx), wide(iu), wide(iv), wide(cu), wide(cv), wide(da_row), wide(da)


def solution(mesh):
    split = P("heads", "rows", None)
    shared = P(None, "rows", None)
    in_specs = (split, split, shared, shared, shared, shared, split, split, P("rows", None))
    return jax.shard_map(body, mesh=mesh, in_specs=in_specs, out_specs=(split,) * 7, check_vma=False)
```
